32 devices in a mesh: strip: 4 (over y, core), cell: 8 (over z, x).
Axes of the slice: x: 2, y: 2, z: 4, core: 2. Of those that a mesh axis runs over, the one named last changes fastest.
Arguments:
- features: bfloat16 [8192, 256], P(('strip', 'cell')), may hold values from -6 to 6
- pair_atom: int32 [131072], P(('strip', 'cell')), may hold values from 0 to 255
- partner_row: int32 [131072], P(('strip', 'cell')), may hold values from 0 to 383, as said below
- transpose_slot: int32 [131072], P(('strip', 'cell')), may hold values from 0 to 6143, as said below
- distance: float32 [131072], P(('strip', 'cell')), may hold values from 1 to 8
- send_rows: int32 [256, 48], P(('strip', 'cell')), may hold values from 0 to 767, as said below
- w_left: bfloat16 [256, 256], replicated, may hold values from -0.375 to 0.375
- w_right: bfloat16 [256, 256], replicated, may hold values from -0.375 to 0.375
- w_radial_in: bfloat16 [128, 256], replicated, may hold values from -4 to 4
- w_radial_out: bfloat16 [256, 256], replicated, may hold values from -0.375 to 0.375
- w_mix: bfloat16 [256, 256], replicated, may hold values from -0.375 to 0.375
- w_out: bfloat16 [256, 169], replicated, may hold values from -0.375 to 0.375
Outputs:
- own_blocks: bfloat16 [169, 131072], P(None, ('strip', 'cell'))
- partner_blocks: bfloat16 [169, 196608], P(None, ('strip', 'cell'))
The draws below stay inside these ranges and needn't reach their ends.
Inputs may be any that keep to these rules, and one draw needn't show every extreme that they name: `transpose_slot`: within one device the values are distinct; at most 256 of them share t // 256, and on every device one such group holds exactly 256. For pair slot p with transpose_slot t: partner_row // 48 equals (t // 256) % 8, and partner_row % 3 equals t // 2048. `send_rows`: entry k lies in [(k % 3) * 256, (k % 3 + 1) * 256); part k % 3 names the device of strip s - 1, s, s + 1 (cyclic) with the same cell index.
All inputs are finite; a program needn't handle non-finite values.
Results may differ from the reference program's by a relative error of at most 0.0084.
Values may be sent and summed in bfloat16 or wider, within the bound.
No kernel may reach another device: no remote copies, remote signals or barrier semaphores. Data moves between devices by JAX's collectives and lax.ppermute only.
A program may use at most 64 MiB of HBM per device.

```python
import jax
import jax.numpy as jnp
import numpy as np
from jax import lax

D = 256
RB = 128
ORB = 13
BLOCK = 169
A_DEV = 256
PAIRS_DEV = 4096
FETCH = 48
SLOT = 256
RECV_DEV = 6144
ATOMS = 8192
PAIRS = 131072
SEND_LISTS = 256
N_STRIP = 4
N_CELL = 8
DEVICES = 32


def pair_tables(key):
    groups = RECV_DEV // SLOT

    def one_device(dev_key):
        first_key, second_key, third_key = jax.random.split(dev_key, 3)
        full_group = jax.random.randint(first_key, (), 0, groups)
        shuffled = jax.random.permutation(second_key, RECV_DEV).astype(jnp.int32)
        slot_group = jnp.arange(RECV_DEV, dtype=jnp.int32) // SLOT
        score = jnp.where(slot_group == full_group, 0, RECV_DEV) + shuffled
        chosen = jnp.argsort(score)[:PAIRS_DEV].astype(jnp.int32)
        offset = chosen // (RECV_DEV // 3)
        source = chosen // SLOT % (groups // 3)
        pick = jax.random.randint(third_key, (PAIRS_DEV,), 0, FETCH // 3)
        return (chosen, (source * FETCH + 3 * pick + offset).astype(jnp.int32))
    keys = jax.random.split(jax.random.fold_in(key, 7), DEVICES)
    return jax.vmap(one_device)(keys)


def draw_transpose_slot(key, part):
    return pair_tables(key)[0].reshape(-1)


def draw_partner_row(key, part):
    return pair_tables(key)[1].reshape(-1)


def draw_send_rows(key, part):
    atom = jax.random.randint(jax.random.fold_in(key, 11), (SEND_LISTS, FETCH), 0, A_DEV)
    return ((jnp.arange(FETCH, dtype=jnp.int32) % 3)[None, :] * A_DEV + atom).astype(jnp.int32)


def place_ends(drawn, stream_key, low, top_value):
    extent = drawn.shape
    place = [jax.random.randint(jax.random.fold_in(stream_key, axis), (), 0, extent[axis]) for axis in range(len(extent))]
    drawn = drawn.at[tuple(place)].set(low)
    longest = extent.index(max(extent))
    place[longest] = (place[longest] + 1) % extent[longest]
    return drawn.at[tuple(place)].set(top_value)


def levels(rng, extent, pieces, smallest, high):
    level, own = 1.0, jax.random.fold_in(rng, 6)
    for dim, blocks in pieces:
        draws = jnp.exp(jax.random.uniform(jax.random.fold_in(own, dim), (blocks,), jnp.float32, smallest / len(pieces), high / len(pieces)))
        level = level * jnp.repeat(draws, extent[dim] // blocks).reshape([-1 if axis == dim else 1 for axis in range(len(extent))])
    return level


def scatter_about(own_key, dims, spread, bound, cuts=(), kind=jnp.bfloat16):
    loudness = levels(own_key, dims, cuts, -0.22, 0.18) if cuts else 1.0
    drawn = jax.random.normal(own_key, dims, jnp.float32) * spread * loudness
    return jnp.minimum(jnp.maximum(drawn, -bound), bound).astype(kind)


def setup_inputs(seed: int = 0) -> dict:
    key_of = jax.random.split(jax.random.key(seed), 13)
    features = scatter_about(key_of[0], (ATOMS, D), 1.0, 6.0, ((0, 32),))
    pair_atom = place_ends(jax.random.randint(key_of[1], (PAIRS,), 0, A_DEV), jax.random.fold_in(key_of[1], 1), 0, A_DEV - 1).astype(jnp.int32)
    partner_row = draw_partner_row(jax.random.fold_in(key_of[12], 71), 0)
    transpose_slot = draw_transpose_slot(jax.random.fold_in(key_of[12], 71), 0)
    distance = jnp.clip(1.0 + 7.0 * jax.random.uniform(key_of[4], (PAIRS,), jnp.float32) ** levels(key_of[4], (PAIRS,), ((0, 32),), -0.2, 0.2), 1.0, 8.0)
    send_rows = draw_send_rows(jax.random.fold_in(key_of[12], 71), 0)
    w_left = scatter_about(key_of[6], (D, D), D ** -0.5, 0.375)
    w_right = scatter_about(key_of[7], (D, D), D ** -0.5, 0.375)
    w_radial_in = scatter_about(key_of[8], (RB, D), 2 ** -0.5, 4.0)
    w_radial_out = scatter_about(key_of[9], (D, D), D ** -0.5, 0.375)
    w_mix = scatter_about(key_of[10], (D, D), D ** -0.5, 0.375)
    w_out = scatter_about(key_of[11], (D, BLOCK), D ** -0.5, 0.375)
    return dict(features=features, pair_atom=pair_atom, partner_row=partner_row, transpose_slot=transpose_slot, distance=distance, send_rows=send_rows, w_left=w_left, w_right=w_right, w_radial_in=w_radial_in, w_radial_out=w_radial_out, w_mix=w_mix, w_out=w_out)


cutoff = 8.0


def radial_basis(distance, count):
    centers = jnp.arange(count, dtype=jnp.float32) * (cutoff / (count - 1))
    spacing = 2.0 * cutoff / count
    scaled = (distance[:, None] - centers[None, :]) / spacing
    envelope = 0.5 * (jnp.cos(jnp.pi * distance / cutoff) + 1.0)
    return (jnp.exp(-scaled * scaled) * envelope[:, None]).astype(jnp.bfloat16)


def pair_blocks(left_rows, right_rows, distance, w_radial_in, w_radial_out, w_mix, w_out):
    basis = radial_basis(distance, w_radial_in.shape[0])
    radial = jax.nn.silu(jnp.dot(basis, w_radial_in, preferred_element_type=jnp.float32)).astype(jnp.bfloat16)
    gate = jnp.dot(radial, w_radial_out, preferred_element_type=jnp.float32)
    edge = (left_rows.astype(jnp.float32) * right_rows.astype(jnp.float32) * gate).astype(jnp.bfloat16)
    mixed = jax.nn.silu(jnp.dot(edge, w_mix, preferred_element_type=jnp.float32)).astype(jnp.bfloat16)
    return lax.dot_general(w_out, mixed, (((0,), (1,)), ((), ())), preferred_element_type=jnp.float32).astype(jnp.bfloat16)


def reference(features, pair_atom, partner_row, transpose_slot, distance, send_rows, w_left, w_right, w_radial_in, w_radial_out, w_mix, w_out):
    devices = N_STRIP * N_CELL
    left_all = jnp.dot(features, w_left, preferred_element_type=jnp.float32).astype(jnp.bfloat16).reshape(N_STRIP, N_CELL, A_DEV, D)
    right_all = jnp.dot(features, w_right, preferred_element_type=jnp.float32).astype(jnp.bfloat16).reshape(N_STRIP, N_CELL, A_DEV, D)
    lists = send_rows.reshape(N_STRIP, N_CELL, N_CELL, FETCH)
    atoms = pair_atom.reshape(devices, PAIRS_DEV)
    partners = partner_row.reshape(devices, PAIRS_DEV)
    spans = distance.reshape(devices, PAIRS_DEV)

    def one_device(index):
        strip_index = index // N_CELL
        column = index % N_CELL
        rows = partners[index]
        source = rows // FETCH
        within = rows % FETCH
        entry = lists[strip_index, source, column, within]
        src_strip = (strip_index + entry // A_DEV - 1) % N_STRIP
        right_rows = right_all[src_strip, source, entry % A_DEV]
        left_rows = left_all[strip_index, column][atoms[index]]
        return pair_blocks(left_rows, right_rows, spans[index], w_radial_in, w_radial_out, w_mix, w_out)

    own_dev = lax.map(one_device, jnp.arange(devices, dtype=jnp.int32))
    own_blocks = own_dev.transpose(1, 0, 2).reshape(BLOCK, devices * PAIRS_DEV)
    order = np.arange(BLOCK).reshape(ORB, ORB).T.reshape(-1)
    flipped = own_blocks[order]
    slots = transpose_slot.reshape(devices, PAIRS_DEV)
    sender = jnp.arange(devices, dtype=jnp.int32)[:, None]
    send_strip = sender // N_CELL
    send_cell = sender % N_CELL
    offset = slots // (N_CELL * SLOT)
    target = (slots // SLOT) % N_CELL
    within_slot = slots % SLOT
    receiver = ((send_strip + offset - 1) % N_STRIP) * N_CELL + target
    columns = receiver * RECV_DEV + offset * (N_CELL * SLOT) + send_cell * SLOT + within_slot
    partner_blocks = jnp.zeros((BLOCK, devices * RECV_DEV), jnp.bfloat16).at[:, columns.reshape(-1).astype(jnp.int32)].set(flipped)
    return own_blocks, partner_blocks
```

```python
import functools

import jax
import jax.numpy as jnp
from jax import lax
from jax.experimental import pallas as pl
from jax.experimental.pallas import tpu as pltpu
from jax.sharding import PartitionSpec as P

cutoff = 8.0
PLANES = 5
BF16 = jnp.bfloat16
F32 = jnp.float32
AXES = ("strip", "cell")


def up(n, by):
    return -(-n // by) * by


def whole_div(x, by):
    return jnp.floor((x.astype(F32) + 0.5) * (1.0 / by)).astype(jnp.int32)


def dot(a, b, ca=1, cb=0):
    return lax.dot_general(a, b, (((ca,), (cb,)), ((), ())), preferred_element_type=F32)


def silu(x):
    half = 0.5 * x
    return half + half * jnp.tanh(half)


def onehot(index, count):
    rows = lax.broadcasted_iota(jnp.int32, (count, index.shape[1]), 0)
    return (rows == index).astype(BF16)


def gate_of(distance, w_in_t, w_out_t):
    count = w_in_t.shape[1]
    centers = lax.broadcasted_iota(jnp.int32, (count, 1), 0).astype(F32) * (cutoff / (count - 1))
    scaled = (distance - centers) * (count / (2.0 * cutoff))
    envelope = 0.5 * (jnp.cos(distance * (jnp.pi / cutoff)) + 1.0)
    basis = (jnp.exp(-scaled * scaled) * envelope).astype(BF16)
    radial = silu(dot(w_in_t, basis)).astype(BF16)
    return dot(w_out_t, radial)


def whole(a):
    return pl.BlockSpec(a.shape, lambda *_: (0,) * a.ndim)


def cost(flops, nbytes=1 << 20):
    return pl.CostEstimate(flops=flops, bytes_accessed=nbytes, transcendentals=0)


class Sizes:
    def __init__(self, features, pair_atom, send_rows, w_radial_in, w_out):
        self.atoms, self.width = features.shape
        self.pairs = pair_atom.shape[0]
        self.cells, self.fetch = send_rows.shape
        self.strips = lax.axis_size("strip")
        self.inner = 2
        self.outer = self.cells // 2
        self.slot = self.pairs // (2 * self.cells)
        self.part = self.fetch // 3
        self.groups = 3 * self.inner
        self.meta = up(PLANES * self.groups, 16)
        self.lists = up(self.cells, 16)
        self.rows = self.atoms + self.meta + self.lists
        self.entries = w_out.shape[1]


def where_am_i():
    strip, cell = lax.axis_index("strip"), lax.axis_index("cell")
    even = lax.rem(strip, 2) == 0
    return cell, lax.div(cell, 2), lax.rem(cell, 2), even


def tiles_kernel(n, atom_ref, row_ref, slot_ref, dist_ref, list_ref, feat_ref, *outs):
    _, zi, _, _ = where_am_i()
    slot = slot_ref[...]
    hi = whole_div(slot, n.slot)
    lo = slot - hi * n.slot
    row = row_ref[...]
    k = row - whole_div(row, n.fetch) * n.fetch
    dist = dist_ref[...]
    d1 = dist.astype(BF16)
    rest = dist - d1.astype(F32)
    d2 = rest.astype(BF16)
    d3 = (rest - d2.astype(F32)).astype(BF16)
    planes = [
        d1.astype(F32),
        d2.astype(F32),
        d3.astype(F32),
        (atom_ref[...] + 1).astype(F32),
        whole_div(k, 3).astype(F32),
    ]
    total = 3 * n.cells
    mask = lax.broadcasted_iota(jnp.int32, (total, n.pairs), 0) == hi
    spread = jnp.concatenate([jnp.where(mask, p, 0.0) for p in planes], 0).astype(BF16)
    placed = dot(spread, onehot(lo, n.slot), 1, 1).astype(BF16)
    shape = (n.meta, PLANES * total)
    r = lax.broadcasted_iota(jnp.int32, shape, 0)
    q = lax.broadcasted_iota(jnp.int32, shape, 1)
    plane = whole_div(r, n.groups)
    g = r - plane * n.groups
    base = plane * total + whole_div(g, n.inner) * n.cells + (g - whole_div(g, n.inner) * n.inner)
    e = list_ref[...]
    kk = lax.broadcasted_iota(jnp.int32, e.shape, 1)
    e = (e - (kk - whole_div(kk, 3) * 3) * n.atoms).astype(F32)
    feat = feat_ref[...]
    for b, out in enumerate(outs):
        zz = jnp.bitwise_xor(zi, b)
        pick = ((base + zz * n.inner == q) & (r < PLANES * n.groups)).astype(BF16)
        out[0 : n.atoms, :] = feat
        tail = dot(pick, placed)
        if n.slot < n.width:
            tail = jnp.concatenate([tail, jnp.zeros((n.meta, n.width - n.slot), F32)], 1)
        out[n.atoms : n.atoms + n.meta, :] = tail.astype(BF16)
        out[n.atoms + n.meta :, :] = jnp.zeros((n.lists, n.width), BF16)
        out[n.atoms + n.meta : n.atoms + n.meta + n.cells, 0 : n.fetch] = e.astype(BF16)


def make_tiles(n, pair_atom, partner_row, transpose_slot, distance, send_rows, features):
    args = (pair_atom, partner_row, transpose_slot, distance, send_rows, features)
    return pl.pallas_call(
        functools.partial(tiles_kernel, n),
        out_shape=[jax.ShapeDtypeStruct((n.rows, n.width), BF16)] * n.outer,
        compiler_params=pltpu.CompilerParams(vmem_limit_bytes=48 << 20),
        cost_estimate=cost(600_000_000),
        name="place_pairs",
    )(*args)


def prepare_kernel(*refs):
    half = len(refs) // 2
    for src, dst in zip(refs[:half], refs[half:]):
        dst[...] = src[...].T


def prepare(weights):
    return pl.pallas_call(
        prepare_kernel,
        out_shape=[jax.ShapeDtypeStruct(w.shape[::-1], w.dtype) for w in weights],
        cost_estimate=cost(100_000_000),
        name="transpose_weights",
    )(*weights)


def own_gate_kernel(dist_ref, atom_ref, feat_ref, w_left_ref, w_in_ref, w_ro_ref, out_ref):
    gate = gate_of(dist_ref[...], w_in_ref[...], w_ro_ref[...])
    left = dot(w_left_ref[...], feat_ref[...], 1, 1).astype(BF16)
    out_ref[...] = gate * dot(left, onehot(atom_ref[...], left.shape[1]))


def own_gate(n, step, distance, pair_atom, features, w_left_t, w_in_t, w_ro_t):
    row = pl.BlockSpec((1, step), lambda i: (0, i))
    return pl.pallas_call(
        own_gate_kernel,
        grid=(n.pairs // step,),
        in_specs=[row, row] + [whole(a) for a in (features, w_left_t, w_in_t, w_ro_t)],
        out_specs=pl.BlockSpec((n.width, step), lambda i: (0, i)),
        out_shape=jax.ShapeDtypeStruct((n.width, n.pairs), F32),
        compiler_params=pltpu.CompilerParams(vmem_limit_bytes=48 << 20),
        cost_estimate=cost(3_000_000_000),
        name="own_gate",
    )(distance, pair_atom, features, w_left_t, w_in_t, w_ro_t)


def partner_tables_kernel(n, own_ref, sib_ref, oth_ref, w_right_ref, out_ref):
    _, _, _, even = where_am_i()
    right = dot(w_right_ref[...], own_ref[0 : n.atoms, :], 1, 1).astype(BF16)
    lanes = n.cells * n.part
    shape = (n.fetch, lanes)
    k = lax.broadcasted_iota(jnp.int32, shape, 0)
    lane = lax.broadcasted_iota(jnp.int32, shape, 1)
    m3 = (lane - whole_div(lane, n.part) * n.part) * 3
    mine = lax.broadcasted_iota(jnp.int32, (n.cells, lanes), 0)
    cell = whole_div(lax.broadcasted_iota(jnp.int32, (n.cells, lanes), 1), n.part)
    o_sib = jnp.where(even, 0, 2)
    for role, (ref, o) in enumerate(((own_ref, 1), (sib_ref, o_sib), (oth_ref, 2 - o_sib))):
        lists = ref[n.atoms + n.meta : n.atoms + n.meta + n.cells, 0 : n.fetch]
        per = dot(lists, (k == m3 + o).astype(BF16))
        index = jnp.sum(jnp.where(mine == cell, per, 0.0), 0, keepdims=True)
        out_ref[role] = dot(right, onehot(index.astype(jnp.int32), n.atoms)).astype(BF16)


def partner_tables(n, own, sib, oth, w_right_t):
    return pl.pallas_call(
        functools.partial(partner_tables_kernel, n),
        out_shape=jax.ShapeDtypeStruct((3, n.width, n.cells * n.part), BF16),
        cost_estimate=cost(200_000_000),
        name="partner_tables",
    )(own, sib, oth, w_right_t)


def received_kernel(n, b, direct, column_ref, *refs):
    tiles, refs = refs[:6], refs[6:]
    table_ref, w_left_ref, w_in_ref, w_ro_ref, w_mix_ref, w_out_ref = refs[:6]
    block_ref, rows_ref = refs[-3:-1] if direct else refs[-2:]
    held = refs[-1] if direct else None

    def compute():
        me, zi, xi, even = where_am_i()
        o_sib = jnp.where(even, 0, 2)
        roles = (1, o_sib, 2 - o_sib)
        r = lax.broadcasted_iota(jnp.int32, (8, n.meta), 0)
        q = lax.broadcasted_iota(jnp.int32, (8, n.meta), 1)
        m3 = 3 * lax.broadcasted_iota(jnp.int32, (n.part, n.fetch), 0)
        k = lax.broadcasted_iota(jnp.int32, (n.part, n.fetch), 1)
        mine = lax.broadcasted_iota(jnp.int32, (n.cells, n.fetch), 0) == me
        metas, lefts, rights = [], [], []
        for at in range(n.inner):
            cell = jnp.bitwise_xor(zi, b) * n.inner + jnp.bitwise_xor(xi, at)
            lists = tiles[3 * at][n.atoms + n.meta : n.atoms + n.meta + n.cells, 0 : n.fetch]
            row = jnp.sum(jnp.where(mine, lists.astype(F32), 0.0), 0, keepdims=True)
            for role, o in enumerate(roles):
                tile = tiles[3 * at + role]
                feat = tile[0 : n.atoms, :]
                here = 3 * at + role
                o_own = 1 if role == 0 else 2 - o
                index = jnp.sum(jnp.where(k == m3 + o_own, row, 0.0), 1, keepdims=True)
                atom = lax.broadcasted_iota(jnp.int32, (n.part, n.atoms), 1)
                pick = (atom == index.astype(jnp.int32)).astype(BF16)
                rows_ref[here * n.part : (here + 1) * n.part, :] = dot(pick, feat).astype(BF16)
                wanted = (q == r * n.groups + o * n.inner + xi) & (r < PLANES)
                meta = dot(wanted.astype(BF16), tile[n.atoms : n.atoms + n.meta, :])
                meta = meta[:, 0 : n.slot]
                left = dot(w_left_ref[...], feat, 1, 1).astype(BF16)
                lefts.append(dot(left, onehot(meta[3:4].astype(jnp.int32) - 1, n.atoms)))
                place = meta[4:5].astype(jnp.int32) + cell * n.part
                rights.append(dot(table_ref[role], onehot(place, n.cells * n.part)))
                metas.append(meta[0:1] + meta[1:2] + meta[2:3])
        gate = gate_of(jnp.concatenate(metas, 1), w_in_ref[...], w_ro_ref[...])
        edge = jnp.concatenate(lefts, 1) * jnp.concatenate(rights, 1) * gate
        mixed = silu(dot(w_mix_ref[...], edge.astype(BF16))).astype(BF16)
        blocks = dot(w_out_ref[...], mixed).astype(BF16)
        if direct:
            for g in range(6):
                held[g] = blocks[:, g * n.slot : (g + 1) * n.slot]
        else:
            block_ref[...] = blocks

    if direct:
        pl.when(pl.program_id(0) == 0)(compute)
        block_ref[...] = held[pl.program_id(0)]
    else:
        compute()


def received(n, b, columns, tiles, table, weights, into):
    direct = n.slot % 128 == 0
    operands = list(tiles) + [table] + list(weights)
    specs = [whole(a) for a in operands]
    aliases = {}
    if direct:
        block = pl.BlockSpec((n.entries, n.slot), lambda i, column: (0, column[i]))
        shape = (n.entries, 3 * n.cells * n.slot)
        scratch = [pltpu.VMEM((6, n.entries, n.slot), BF16)]
        if into is not None:
            aliases = {1 + len(operands): 0}
            operands.append(into)
            specs.append(pl.BlockSpec(memory_space=pl.ANY))
    else:
        shape = (n.entries, 6 * n.slot)
        block = pl.BlockSpec(shape, lambda i, column: (0, 0))
        scratch = []
    rows = (6 * n.part, n.width)
    return pl.pallas_call(
        functools.partial(received_kernel, n, b, direct),
        grid_spec=pltpu.PrefetchScalarGridSpec(
            num_scalar_prefetch=1,
            grid=(6 if direct else 1,),
            in_specs=specs,
            out_specs=[block, pl.BlockSpec(rows, lambda i, column: (0, 0))],
            scratch_shapes=scratch,
        ),
        out_shape=[jax.ShapeDtypeStruct(shape, BF16), jax.ShapeDtypeStruct(rows, BF16)],
        input_output_aliases=aliases,
        compiler_params=pltpu.CompilerParams(vmem_limit_bytes=48 << 20),
        cost_estimate=cost(3_000_000_000),
        name="received_blocks",
    )(columns, *operands)


def own_blocks_kernel(n, row_ref, held_ref, w_right_ref, w_mix_ref, w_out_ref, *refs):
    tables, out_ref, right_ref = refs[:-2], refs[-2], refs[-1]
    _, zi, xi, even = where_am_i()

    @pl.when(pl.program_id(0) == 0)
    def _():
        rows = jnp.concatenate([t[...] for t in tables], 0)
        right_ref[...] = dot(w_right_ref[...], rows, 1, 1).astype(BF16)

    v = row_ref[...]
    q = whole_div(v, n.fetch)
    k = v - q * n.fetch
    m = whole_div(k, 3)
    o = k - 3 * m
    sibling = jnp.where(even, 2, 0)
    role = jnp.where(o == 1, 0, jnp.where(o == sibling, 1, 2))
    outer = whole_div(q, n.inner)
    inner = q - outer * n.inner
    place = (jnp.bitwise_xor(outer, zi) * n.inner + jnp.bitwise_xor(inner, xi)) * 3 + role
    right = dot(right_ref[...], onehot(place * n.part + m, right_ref.shape[1]))
    edge = (held_ref[...] * right).astype(BF16)
    mixed = silu(dot(w_mix_ref[...], edge)).astype(BF16)
    out_ref[...] = dot(w_out_ref[...], mixed).astype(BF16)


def own_blocks_of(n, step, partner_row, held, w_right_t, w_mix_t, w_out_t, tables):
    return pl.pallas_call(
        functools.partial(own_blocks_kernel, n),
        grid=(n.pairs // step,),
        in_specs=[
            pl.BlockSpec((1, step), lambda i: (0, i)),
            pl.BlockSpec((n.width, step), lambda i: (0, i)),
        ]
        + [whole(a) for a in (w_right_t, w_mix_t, w_out_t, *tables)],
        out_specs=pl.BlockSpec((n.entries, step), lambda i: (0, i)),
        out_shape=jax.ShapeDtypeStruct((n.entries, n.pairs), BF16),
        scratch_shapes=[pltpu.VMEM((n.width, 3 * n.cells * n.part), BF16)],
        compiler_params=pltpu.CompilerParams(vmem_limit_bytes=48 << 20),
        cost_estimate=cost(3_000_000_000),
        name="own_blocks",
    )(partner_row, held, w_right_t, w_mix_t, w_out_t, *tables)


def body(
    features,
    pair_atom,
    partner_row,
    transpose_slot,
    distance,
    send_rows,
    w_left,
    w_right,
    w_radial_in,
    w_radial_out,
    w_mix,
    w_out,
):
    n = Sizes(features, pair_atom, send_rows, w_radial_in, w_out)
    orbitals = int(n.entries**0.5 + 0.5)
    lines = n.strips * n.cells

    def exchange(x, partner):
        pairs = []
        for i in range(lines):
            s, c = partner(i // n.cells, i % n.cells)
            pairs.append((i, s * n.cells + c))
        return lax.ppermute(x, AXES, pairs)

    def along(by):
        return lambda s, c: (s, c ^ (by * n.inner))

    def beside(s, c):
        return s, c ^ 1

    def sibling(s, c):
        return s ^ 1, c

    def other(s, c):
        return (s - 1 if s % 2 == 0 else s + 1) % n.strips, c

    def corner(s, c):
        return other(s, c)[0], c ^ 1

    row = lambda a: a.reshape(1, -1)
    pair_atom, partner_row = row(pair_atom), row(partner_row)
    transpose_slot, distance = row(transpose_slot), row(distance)
    tiles = make_tiles(
        n, pair_atom, partner_row, transpose_slot, distance, send_rows, features
    )
    lines_in = [tiles[0]] + [exchange(tiles[b], along(b)) for b in range(1, n.outer)]
    flip = w_out.reshape(-1, orbitals, orbitals).swapaxes(1, 2).reshape(w_out.shape)
    w_left_t, w_right_t, w_in_t, w_ro_t, w_mix_t, w_out_t, w_flip_t = prepare(
        [w_left, w_right, w_radial_in, w_radial_out, w_mix, w_out, flip]
    )
    step = n.pairs // 2
    held = own_gate(n, step, distance, pair_atom, features, w_left_t, w_in_t, w_ro_t)
    cell = lax.axis_index("cell")
    strip = lax.axis_index("strip")
    o_sib = jnp.where(strip % 2 == 0, 0, 2)
    weights = (w_left_t, w_in_t, w_ro_t, w_mix_t, w_flip_t)
    table, into, tables, parts = None, None, [], []
    for b, tile in enumerate(lines_in):
        across = exchange(tile, beside)
        group = [
            tile,
            exchange(tile, sibling),
            exchange(tile, other),
            across,
            exchange(across, sibling),
            exchange(tile, corner),
        ]
        if b == 0:
            table = partner_tables(n, group[0], group[1], group[2], w_right_t)
        near = cell ^ (b * n.inner)
        columns = jnp.stack(
            [o * n.cells + c for c in (near, near ^ 1) for o in (1, o_sib, 2 - o_sib)]
        ).astype(jnp.int32)
        into, rows = received(n, b, columns, group, table, weights, into)
        tables.append(rows)
        parts.append((columns, into))
    if n.slot % 128:
        into = jnp.zeros((n.entries, 3 * n.cells * n.slot), BF16)
        for columns, blocks in parts:
            for g in range(6):
                piece = blocks[:, g * n.slot : (g + 1) * n.slot]
                into = lax.dynamic_update_slice(into, piece, (0, columns[g] * n.slot))
    own = own_blocks_of(n, step, partner_row, held, w_right_t, w_mix_t, w_out_t, tables)
    return own, into


def solution(mesh):
    split = P(("strip", "cell"))
    wide = P(("strip", "cell"), None)
    in_specs = (wide, split, split, split, split, wide) + (P(),) * 6
    out_specs = (P(None, ("strip", "cell")), P(None, ("strip", "cell")))
    return jax.shard_map(body, mesh=mesh, in_specs=in_specs, out_specs=out_specs, check_vma=False)
```

```python
import functools

import jax
import jax.numpy as jnp
from jax import lax
from jax.experimental import pallas as pl
from jax.experimental.pallas import tpu as pltpu
from jax.sharding import PartitionSpec as P

cutoff = 8.0
PLANES = 5
LIST = 64
LIMIT = 36 << 20
BF16 = jnp.bfloat16
F32 = jnp.float32
AXES = ("strip", "cell")


def up(n, by):
    return -(-n // by) * by


def whole_div(x, by):
    return jnp.floor((x.astype(F32) + 0.5) * (1.0 / by)).astype(jnp.int32)


def dot(a, b, ca=1, cb=0):
    return lax.dot_general(a, b, (((ca,), (cb,)), ((), ())), preferred_element_type=F32)


def silu(x):
    half = 0.5 * x
    return half + half * jnp.tanh(half)


def onehot(index, count):
    rows = lax.broadcasted_iota(jnp.int32, (count, index.shape[1]), 0)
    return (rows == index).astype(BF16)


def gate_of(distance, w_in_t, w_out_t):
    count = w_in_t.shape[1]
    centers = lax.broadcasted_iota(jnp.int32, (count, 1), 0).astype(F32) * (cutoff / (count - 1))
    scaled = (distance - centers) * (count / (2.0 * cutoff))
    envelope = 0.5 * (jnp.cos(distance * (jnp.pi / cutoff)) + 1.0)
    basis = (jnp.exp(-scaled * scaled) * envelope).astype(BF16)
    radial = silu(dot(w_in_t, basis)).astype(BF16)
    return dot(w_out_t, radial)


def whole(a):
    return pl.BlockSpec(a.shape, lambda *_: (0,) * a.ndim)


def far(*arrays):
    return [pltpu.with_memory_space_constraint(a, pltpu.HBM) for a in arrays]


def cost(flops, nbytes=1 << 20):
    return pl.CostEstimate(flops=flops, bytes_accessed=nbytes, transcendentals=0)


class Sizes:
    def __init__(self, features, pair_atom, send_rows, w_radial_in, w_out):
        self.atoms, self.width = features.shape
        self.pairs = pair_atom.shape[0]
        self.cells, self.fetch = send_rows.shape
        self.strips = lax.axis_size("strip")
        self.inner = 2
        self.outer = self.cells // 2
        self.slot = self.pairs // (2 * self.cells)
        self.part = self.fetch // 3
        self.groups = 3 * self.inner
        self.meta = PLANES * self.groups
        self.per_row = self.width // LIST
        self.rows = up(self.atoms + self.meta + -(-self.cells // self.per_row), 16)
        self.entries = w_out.shape[1]
        self.orbitals = int(self.entries**0.5 + 0.5)


def where_am_i():
    strip, cell = lax.axis_index("strip"), lax.axis_index("cell")
    even = lax.rem(strip, 2) == 0
    return cell, lax.div(cell, 2), lax.rem(cell, 2), even


def tiles_kernel(n, atom_ref, row_ref, slot_ref, dist_ref, list_ref, feat_ref, *outs):
    _, zi, xi, even = where_am_i()
    slot = slot_ref[...]
    hi = whole_div(slot, n.slot)
    lo = slot - hi * n.slot
    row = row_ref[...]
    k = row - whole_div(row, n.fetch) * n.fetch
    dist = dist_ref[...]
    d1 = dist.astype(BF16)
    rest = dist - d1.astype(F32)
    d2 = rest.astype(BF16)
    d3 = (rest - d2.astype(F32)).astype(BF16)
    planes = [
        d1.astype(F32),
        d2.astype(F32),
        d3.astype(F32),
        (atom_ref[...] + 1).astype(F32),
        whole_div(k, 3).astype(F32),
    ]
    total = 3 * n.cells
    mask = lax.broadcasted_iota(jnp.int32, (total, n.pairs), 0) == hi
    spread = jnp.concatenate([jnp.where(mask, p, 0.0) for p in planes], 0).astype(BF16)
    placed = dot(spread, onehot(lo, n.slot), 1, 1).astype(BF16)
    tail = n.rows - n.atoms
    shape = (tail, PLANES * total)
    r = lax.broadcasted_iota(jnp.int32, shape, 0)
    q = lax.broadcasted_iota(jnp.int32, shape, 1)
    g = whole_div(r, PLANES)
    plane = r - g * PLANES
    role = whole_div(g, n.inner)
    o = jnp.where(role == 0, 1, jnp.where((role == 1) == even, 2, 0))
    base = plane * total + o * n.cells + jnp.bitwise_xor(g - role * n.inner, xi)
    base = jnp.where(r < n.meta, base, -n.pairs)
    e = list_ref[...]
    kk = lax.broadcasted_iota(jnp.int32, e.shape, 1)
    e = (e - (kk - whole_div(kk, 3) * 3) * n.atoms).astype(F32)
    wide = jnp.concatenate([e, jnp.zeros((n.cells, LIST - n.fetch), F32)], 1)
    flat = jnp.concatenate([wide] * n.per_row, 1)
    j = lax.broadcasted_iota(jnp.int32, flat.shape, 0)
    lane = lax.broadcasted_iota(jnp.int32, flat.shape, 1)
    at_row = whole_div(j, n.per_row)
    flat = jnp.where(whole_div(lane, LIST) == j - at_row * n.per_row, flat, 0.0).astype(BF16)
    put_r = lax.broadcasted_iota(jnp.int32, (tail, n.cells), 0)
    put_j = lax.broadcasted_iota(jnp.int32, (tail, n.cells), 1)
    put = (put_r == n.meta + whole_div(put_j, n.per_row)).astype(BF16)
    lists = dot(put, flat)
    feat = feat_ref[...]
    for b, out in enumerate(outs):
        zz = jnp.bitwise_xor(zi, b)
        pick = (base + zz * n.inner == q).astype(BF16)
        out[0 : n.atoms, :] = feat
        pairs = dot(pick, placed)
        if n.slot < n.width:
            pairs = jnp.concatenate([pairs, jnp.zeros((tail, n.width - n.slot), F32)], 1)
        out[n.atoms :, :] = (pairs + lists).astype(BF16)


def lists_of(n, tile):
    tail = tile[n.atoms :, :].astype(F32)
    rows = []
    for j in range(n.cells):
        r = n.meta + j // n.per_row
        lane = LIST * (j % n.per_row)
        rows.append(tail[r : r + 1, lane : lane + n.fetch])
    return jnp.concatenate(rows, 0)


def make_tiles(n, pair_atom, partner_row, transpose_slot, distance, send_rows, features):
    args = (pair_atom, partner_row, transpose_slot, distance, send_rows, features)
    return pl.pallas_call(
        functools.partial(tiles_kernel, n),
        out_shape=[jax.ShapeDtypeStruct((n.rows, n.width), BF16)] * n.outer,
        compiler_params=pltpu.CompilerParams(vmem_limit_bytes=LIMIT),
        cost_estimate=cost(600_000_000),
        name="place_pairs",
    )(*far(*args))


def own_gate_kernel(n, dist_ref, atom_ref, feat_ref, *refs):
    sources, held_ref, flipped, left_ref = refs[:6], refs[6], refs[7:13], refs[13]

    @pl.when(pl.program_id(0) == 0)
    def _():
        for src, dst in zip(sources[:5], flipped[:5]):
            dst[...] = src[...].T
        r = lax.broadcasted_iota(jnp.int32, (n.entries, n.entries), 0)
        q = lax.broadcasted_iota(jnp.int32, (n.entries, n.entries), 1)
        first = whole_div(r, n.orbitals)
        swap = (q == (r - first * n.orbitals) * n.orbitals + first).astype(BF16)
        flipped[5][...] = dot(swap, sources[5][...]).astype(BF16)
        left_ref[...] = dot(flipped[0][...], feat_ref[...], 1, 1).astype(BF16)

    gate = gate_of(dist_ref[...], flipped[2][...], flipped[3][...])
    held_ref[...] = gate * dot(left_ref[...], onehot(atom_ref[...], n.atoms))


def own_gate(n, step, distance, pair_atom, features, weights):
    row = pl.BlockSpec((1, step), lambda i: (0, i))
    turned = [jax.ShapeDtypeStruct(w.shape[::-1], BF16) for w in weights[:5]]
    turned.append(jax.ShapeDtypeStruct(weights[5].shape, BF16))
    out = pl.pallas_call(
        functools.partial(own_gate_kernel, n),
        grid=(n.pairs // step,),
        in_specs=[row, row] + [whole(a) for a in (features, *weights)],
        out_specs=[pl.BlockSpec((n.width, step), lambda i: (0, i))] + [whole(a) for a in turned],
        out_shape=[jax.ShapeDtypeStruct((n.width, n.pairs), F32)] + turned,
        scratch_shapes=[pltpu.VMEM((n.width, n.atoms), BF16)],
        compiler_params=pltpu.CompilerParams(vmem_limit_bytes=LIMIT),
        cost_estimate=cost(3_000_000_000),
        name="own_gate",
    )(*far(distance, pair_atom, features, *weights))
    return out[0], out[1:]


def partner_table(n, even, tiles, w_right_t, table_ref):
    right = dot(w_right_t, tiles[0][0 : n.atoms, :], 1, 1).astype(BF16)
    lanes = n.cells * n.part
    k = lax.broadcasted_iota(jnp.int32, (n.fetch, lanes), 0)
    lane = lax.broadcasted_iota(jnp.int32, (n.fetch, lanes), 1)
    m3 = (lane - whole_div(lane, n.part) * n.part) * 3
    mine = lax.broadcasted_iota(jnp.int32, (n.cells, lanes), 0)
    cell = whole_div(lax.broadcasted_iota(jnp.int32, (n.cells, lanes), 1), n.part)
    o_sib = jnp.where(even, 0, 2)
    for role, o in enumerate((1, o_sib, 2 - o_sib)):
        lists = lists_of(n, tiles[role]).astype(BF16)
        per = dot(lists, (k == m3 + o).astype(BF16))
        index = jnp.sum(jnp.where(mine == cell, per, 0.0), 0, keepdims=True)
        table_ref[role] = dot(right, onehot(index.astype(jnp.int32), n.atoms)).astype(BF16)


def received_kernel(n, steps, first, direct, count, *refs):
    held, refs = refs[:count], refs[count:]
    if not first and direct:
        refs = refs[1:]
    outs, refs = refs[: 3 if first else 2], refs[3 if first else 2 :]
    blocks_buf, sem_out = refs
    block_ref, rows_buf = outs[:2]
    need = held.__getitem__

    me, zi, xi, even = where_am_i()
    o_sib = jnp.where(even, 0, 2)
    roles = (1, o_sib, 2 - o_sib)
    base = 6 * len(steps)
    near = [(i, at) for i in range(len(steps)) for at in range(n.inner)]
    order = [(role, i, at) for role in range(3) for i, at in near]
    number = {key: g for g, key in enumerate(order)}
    cells = {
        (i, at): jnp.bitwise_xor(zi, steps[i]) * n.inner + jnp.bitwise_xor(xi, at) for i, at in near
    }
    tiles = {(role, i, at): need(6 * i + 3 * at + role) for role, i, at in order}
    done = []
    if first:
        own = [tiles[role, 0, 0] for role in range(3)]
        table = outs[2]
        partner_table(n, even, own, need(base + 5)[...], table)
    else:
        table = need(base + 5)
    feats = jnp.concatenate([tiles[key][0 : n.atoms, :] for key in order], 0)
    left = dot(need(base)[...], feats, 1, 1).astype(BF16)

    slabs = []
    for role, i, at in order:
        top = (role * n.inner + at) * PLANES
        tail = tiles[role, i, at][n.atoms :, 0 : n.slot].astype(F32)
        slabs.append(tail[top : top + PLANES])
    meta = jnp.concatenate(slabs, 1)
    dists = meta[0:1] + meta[1:2] + meta[2:3]
    atoms = meta[3:4].astype(jnp.int32) - 1
    spots = meta[4:5].astype(jnp.int32)

    def cut(x, g):
        return x[:, g * n.slot : (g + 1) * n.slot]

    gate = gate_of(dists, need(base + 1)[...], need(base + 2)[...])
    rights = []
    for role in range(3):
        place = [cut(spots, number[role, i, at]) + cells[i, at] * n.part for i, at in near]
        rights.append(dot(table[role], onehot(jnp.concatenate(place, 1), n.cells * n.part)))
    lefts = [
        dot(left[:, g * n.atoms : (g + 1) * n.atoms], onehot(cut(atoms, g), n.atoms))
        for g in range(len(order))
    ]
    edge = jnp.concatenate(lefts, 1) * jnp.concatenate(rights, 1) * gate
    mixed = silu(dot(need(base + 3)[...], edge.astype(BF16))).astype(BF16)
    blocks_buf[...] = dot(need(base + 4)[...], mixed).astype(BF16)
    if direct:
        for g, (role, i, at) in enumerate(order):
            place = roles[role] * n.cells + cells[i, at]
            start = pl.multiple_of(place * n.slot, n.slot)
            out = pltpu.make_async_copy(
                blocks_buf.at[:, pl.ds(g * n.slot, n.slot)],
                block_ref.at[:, pl.ds(start, n.slot)],
                sem_out.at[g],
            )
            out.start()
            done.append(out)

    rows = len(order) * n.part
    mine = lax.broadcasted_iota(jnp.int32, (n.cells, n.fetch), 0) == me
    index = []
    k = lax.broadcasted_iota(jnp.int32, (n.part, n.fetch), 1)
    m3 = 3 * lax.broadcasted_iota(jnp.int32, (n.part, n.fetch), 0)
    asked = {}
    for i, at in near:
        lists = lists_of(n, tiles[0, i, at])
        asked[i, at] = jnp.sum(jnp.where(mine, lists, 0.0), 0, keepdims=True)
    for g, (role, i, at) in enumerate(order):
        o_own = 1 if role == 0 else 2 - roles[role]
        here = jnp.sum(jnp.where(k == m3 + o_own, asked[i, at], 0.0), 1, keepdims=True)
        index.append(here.astype(jnp.int32) + g * n.atoms)
    lane = lax.broadcasted_iota(jnp.int32, (rows, len(order) * n.atoms), 1)
    pick = (lane == jnp.concatenate(index, 0)).astype(BF16)
    rows_buf[...] = dot(pick, feats).astype(BF16)
    if not direct:
        out = pltpu.make_async_copy(blocks_buf, block_ref, sem_out.at[0])
        out.start()
        done.append(out)
    for out in done:
        out.wait()


def received(n, steps, tiles, weights, table, w_right_t, into):
    first = table is None
    direct = n.slot % 128 == 0
    operands = list(tiles) + list(weights) + [w_right_t if first else table]
    count = len(operands)
    blocks = (n.entries, 6 * len(steps) * n.slot)
    rows = (6 * len(steps) * n.part, n.width)
    shape = (3, n.width, n.cells * n.part)
    out_shape = [
        jax.ShapeDtypeStruct((n.entries, 3 * n.cells * n.slot) if direct else blocks, BF16),
        jax.ShapeDtypeStruct(rows, BF16),
    ]
    if first:
        out_shape.append(jax.ShapeDtypeStruct(shape, BF16))
    aliases = {}
    if direct and not first:
        aliases = {count: 0}
        operands.append(into)
    out = pl.pallas_call(
        functools.partial(received_kernel, n, steps, first, direct, count),
        in_specs=[pl.BlockSpec(memory_space=pltpu.VMEM)] * count + [pl.BlockSpec(memory_space=pl.ANY)] * (len(operands) - count),
        out_specs=[pl.BlockSpec(memory_space=pl.ANY)] + [pl.BlockSpec(memory_space=pltpu.VMEM)] * (len(out_shape) - 1),
        out_shape=out_shape,
        scratch_shapes=[
            pltpu.VMEM(blocks, BF16),
            pltpu.SemaphoreType.DMA((6 * len(steps),)),
        ],
        input_output_aliases=aliases,
        compiler_params=pltpu.CompilerParams(vmem_limit_bytes=LIMIT),
        cost_estimate=cost(3_000_000_000 * len(steps)),
        name="received_blocks",
    )(*operands)
    return out[0], out[1], out[2] if first else table


def own_blocks_kernel(n, per_call, row_ref, held_ref, w_right_ref, w_mix_ref, w_out_ref, *refs):
    tables, out_ref, right_ref = refs[:-2], refs[-2], refs[-1]
    _, zi, xi, even = where_am_i()

    @pl.when(pl.program_id(0) == 0)
    def _():
        rows = jnp.concatenate([t[...] for t in tables], 0)
        right_ref[...] = dot(w_right_ref[...], rows, 1, 1).astype(BF16)

    v = row_ref[...]
    q = whole_div(v, n.fetch)
    k = v - q * n.fetch
    m = whole_div(k, 3)
    o = k - 3 * m
    sibling = jnp.where(even, 2, 0)
    role = jnp.where(o == 1, 0, jnp.where(o == sibling, 1, 2))
    outer = whole_div(q, n.inner)
    inner = q - outer * n.inner
    b = jnp.bitwise_xor(outer, zi)
    call = whole_div(b, per_call)
    place = (call * 3 + role) * per_call + b - call * per_call
    place = place * n.inner + jnp.bitwise_xor(inner, xi)
    right = dot(right_ref[...], onehot(place * n.part + m, right_ref.shape[1]))
    edge = (held_ref[...] * right).astype(BF16)
    mixed = silu(dot(w_mix_ref[...], edge)).astype(BF16)
    out_ref[...] = dot(w_out_ref[...], mixed).astype(BF16)


def own_blocks_of(n, step, partner_row, held, w_right_t, w_mix_t, w_out_t, tables):
    return pl.pallas_call(
        functools.partial(own_blocks_kernel, n, n.outer // len(tables)),
        grid=(n.pairs // step,),
        in_specs=[
            pl.BlockSpec((1, step), lambda i: (0, i)),
            pl.BlockSpec((n.width, step), lambda i: (0, i)),
        ]
        + [whole(a) for a in (w_right_t, w_mix_t, w_out_t, *tables)],
        out_specs=pl.BlockSpec((n.entries, step), lambda i: (0, i)),
        out_shape=jax.ShapeDtypeStruct((n.entries, n.pairs), BF16),
        scratch_shapes=[pltpu.VMEM((n.width, 3 * n.cells * n.part), BF16)],
        compiler_params=pltpu.CompilerParams(vmem_limit_bytes=LIMIT),
        cost_estimate=cost(3_000_000_000),
        name="own_blocks",
    )(*far(partner_row), held, w_right_t, w_mix_t, w_out_t, *tables)


def body(
    features,
    pair_atom,
    partner_row,
    transpose_slot,
    distance,
    send_rows,
    w_left,
    w_right,
    w_radial_in,
    w_radial_out,
    w_mix,
    w_out,
):
    n = Sizes(features, pair_atom, send_rows, w_radial_in, w_out)
    lines = n.strips * n.cells

    def exchange(x, partner):
        pairs = []
        for i in range(lines):
            s, c = partner(i // n.cells, i % n.cells)
            pairs.append((i, s * n.cells + c))
        return lax.ppermute(x, AXES, pairs)

    def along(by):
        return lambda s, c: (s, c ^ (by * n.inner))

    def beside(s, c):
        return s, c ^ 1

    def sibling(s, c):
        return s ^ 1, c

    def other(s, c):
        return (s - 1 if s % 2 == 0 else s + 1) % n.strips, c

    def corner(s, c):
        return other(s, c)[0], c ^ 1

    row = lambda a: a.reshape(1, -1)
    pair_atom, partner_row = row(pair_atom), row(partner_row)
    transpose_slot, distance = row(transpose_slot), row(distance)
    tiles = make_tiles(
        n, pair_atom, partner_row, transpose_slot, distance, send_rows, features
    )
    lines_in = [tiles[0]] + [exchange(tiles[b], along(b)) for b in range(1, n.outer)]
    step = n.pairs // 2
    held, turned = own_gate(
        n,
        step,
        distance,
        pair_atom,
        features,
        (w_left, w_right, w_radial_in, w_radial_out, w_mix, w_out.T),
    )
    w_left_t, w_right_t, w_in_t, w_ro_t, w_mix_t, w_flip_t = turned
    weights = (w_left_t, w_in_t, w_ro_t, w_mix_t, w_flip_t)
    table, into, tables, parts = None, None, [], []
    half = 1
    for at in range(0, n.outer, half):
        steps, group = tuple(range(at, at + half)), []
        for b in steps:
            tile = lines_in[b]
            across = exchange(tile, beside)
            group += [
                tile,
                exchange(tile, sibling),
                exchange(tile, other),
                across,
                exchange(across, sibling),
                exchange(tile, corner),
            ]
        into, rows, table = received(n, steps, group, weights, table, w_right_t, into)
        tables.append(rows)
        parts.append((steps, into))
    if n.slot % 128:
        cell, strip = lax.axis_index("cell"), lax.axis_index("strip")
        o_sib = jnp.where(strip % 2 == 0, 0, 2)
        into = jnp.zeros((n.entries, 3 * n.cells * n.slot), BF16)
        for steps, blocks in parts:
            order = [(o, b, at) for o in (1, o_sib, 2 - o_sib) for b in steps for at in (0, 1)]
            for g, (o, b, at) in enumerate(order):
                piece = blocks[:, g * n.slot : (g + 1) * n.slot]
                spot = o * n.cells + (cell ^ (b * n.inner + at))
                into = lax.dynamic_update_slice(into, piece, (0, spot * n.slot))
    own = own_blocks_of(n, step, partner_row, held, w_right_t, w_mix_t, w_out.T, tables)
    return own, into


def solution(mesh):
    split = P(("strip", "cell"))
    wide = P(("strip", "cell"), None)
    in_specs = (wide, split, split, split, split, wide) + (P(),) * 6
    out_specs = (P(None, ("strip", "cell")), P(None, ("strip", "cell")))
    return jax.shard_map(body, mesh=mesh, in_specs=in_specs, out_specs=out_specs, check_vma=False)
```

```python
import functools

import jax
import jax.numpy as jnp
from jax import lax
from jax.experimental import pallas as pl
from jax.experimental.pallas import tpu as pltpu
from jax.sharding import PartitionSpec as P

cutoff = 8.0
PLANES = 5
LIST = 64
LIMIT = 36 << 20
BF16 = jnp.bfloat16
F32 = jnp.float32
AXES = ("strip", "cell")


def up(n, by):
    return -(-n // by) * by


def whole_div(x, by):
    return jnp.floor((x.astype(F32) + 0.5) * (1.0 / by)).astype(jnp.int32)


def dot(a, b, ca=1, cb=0):
    return lax.dot_general(a, b, (((ca,), (cb,)), ((), ())), preferred_element_type=F32)


def silu(x):
    half = 0.5 * x
    return half + half * jnp.tanh(half)


def onehot(index, count):
    rows = lax.broadcasted_iota(jnp.int32, (count, index.shape[1]), 0)
    return (rows == index).astype(BF16)


def gate_of(distance, w_in_t, w_out_t):
    count = w_in_t.shape[1]
    centers = lax.broadcasted_iota(jnp.int32, (count, 1), 0).astype(F32) * (cutoff / (count - 1))
    scaled = (distance - centers) * (count / (2.0 * cutoff))
    envelope = 0.5 * (jnp.cos(distance * (jnp.pi / cutoff)) + 1.0)
    basis = (jnp.exp(-scaled * scaled) * envelope).astype(BF16)
    radial = silu(dot(w_in_t, basis)).astype(BF16)
    return dot(w_out_t, radial)


def whole(a):
    return pl.BlockSpec(a.shape, lambda *_: (0,) * a.ndim)


def far(*arrays):
    return [pltpu.with_memory_space_constraint(a, pltpu.HBM) for a in arrays]


def cost(flops, nbytes=1 << 20):
    return pl.CostEstimate(flops=flops, bytes_accessed=nbytes, transcendentals=0)


class Sizes:
    def __init__(self, features, pair_atom, send_rows, w_radial_in, w_out):
        self.atoms, self.width = features.shape
        self.pairs = pair_atom.shape[0]
        self.cells, self.fetch = send_rows.shape
        self.strips = lax.axis_size("strip")
        self.inner = 2
        self.outer = self.cells // 2
        self.slot = self.pairs // (2 * self.cells)
        self.part = self.fetch // 3
        self.groups = 3 * self.inner
        self.section = PLANES * self.groups
        self.meta = 2 * self.section
        self.per_row = self.width // LIST
        self.rows = up(self.atoms + self.meta + -(-self.cells // self.per_row), 16)
        self.entries = w_out.shape[1]
        self.orbitals = int(self.entries**0.5 + 0.5)


def where_am_i():
    strip, cell = lax.axis_index("strip"), lax.axis_index("cell")
    even = lax.rem(strip, 2) == 0
    return cell, lax.div(cell, 2), lax.rem(cell, 2), even


def sent_steps(n):
    return [b for b in range(n.outer) if b < 2 or b % 2 == 0]


def tiles_kernel(n, atom_ref, row_ref, slot_ref, dist_ref, list_ref, feat_ref, *outs):
    _, zi, xi, even = where_am_i()
    slot = slot_ref[...]
    hi = whole_div(slot, n.slot)
    lo = slot - hi * n.slot
    row = row_ref[...]
    k = row - whole_div(row, n.fetch) * n.fetch
    dist = dist_ref[...]
    d1 = dist.astype(BF16)
    rest = dist - d1.astype(F32)
    d2 = rest.astype(BF16)
    d3 = (rest - d2.astype(F32)).astype(BF16)
    planes = [
        d1.astype(F32),
        d2.astype(F32),
        d3.astype(F32),
        (atom_ref[...] + 1).astype(F32),
        whole_div(k, 3).astype(F32),
    ]
    total = 3 * n.cells
    mask = lax.broadcasted_iota(jnp.int32, (total, n.pairs), 0) == hi
    spread = jnp.concatenate([jnp.where(mask, p, 0.0) for p in planes], 0).astype(BF16)
    placed = dot(spread, onehot(lo, n.slot), 1, 1).astype(BF16)
    tail = n.rows - n.atoms
    shape = (tail, PLANES * total)
    r = lax.broadcasted_iota(jnp.int32, shape, 0)
    q = lax.broadcasted_iota(jnp.int32, shape, 1)
    section = whole_div(r, n.section)
    g = whole_div(r - section * n.section, PLANES)
    plane = r - section * n.section - g * PLANES
    role = whole_div(g, n.inner)
    o = jnp.where(role == 0, 1, jnp.where((role == 1) == even, 2, 0))
    base = plane * total + o * n.cells + jnp.bitwise_xor(g - role * n.inner, xi)
    base = jnp.where(r < n.meta, base, -n.pairs)
    section = jnp.where(r < n.meta, section, 0)
    e = list_ref[...]
    kk = lax.broadcasted_iota(jnp.int32, e.shape, 1)
    e = (e - (kk - whole_div(kk, 3) * 3) * n.atoms).astype(F32)
    wide = jnp.concatenate([e, jnp.zeros((n.cells, LIST - n.fetch), F32)], 1)
    flat = jnp.concatenate([wide] * n.per_row, 1)
    j = lax.broadcasted_iota(jnp.int32, flat.shape, 0)
    lane = lax.broadcasted_iota(jnp.int32, flat.shape, 1)
    at_row = whole_div(j, n.per_row)
    flat = jnp.where(whole_div(lane, LIST) == j - at_row * n.per_row, flat, 0.0).astype(BF16)
    put_r = lax.broadcasted_iota(jnp.int32, (tail, n.cells), 0)
    put_j = lax.broadcasted_iota(jnp.int32, (tail, n.cells), 1)
    put = (put_r == n.meta + whole_div(put_j, n.per_row)).astype(BF16)
    lists = dot(put, flat)
    feat = feat_ref[...]
    for b, out in zip(sent_steps(n), outs):
        plane_of = jnp.bitwise_xor(jnp.bitwise_xor(zi, b), section)
        pick = (base + plane_of * n.inner == q).astype(BF16)
        out[0 : n.atoms, :] = feat
        pairs = dot(pick, placed)
        if n.slot < n.width:
            pairs = jnp.concatenate([pairs, jnp.zeros((tail, n.width - n.slot), F32)], 1)
        out[n.atoms :, :] = (pairs + lists).astype(BF16)


def lists_of(n, tile):
    tail = tile[n.atoms :, :].astype(F32)
    rows = []
    for j in range(n.cells):
        r = n.meta + j // n.per_row
        lane = LIST * (j % n.per_row)
        rows.append(tail[r : r + 1, lane : lane + n.fetch])
    return jnp.concatenate(rows, 0)


def make_tiles(n, pair_atom, partner_row, transpose_slot, distance, send_rows, features):
    args = (pair_atom, partner_row, transpose_slot, distance, send_rows, features)
    return pl.pallas_call(
        functools.partial(tiles_kernel, n),
        out_shape=[jax.ShapeDtypeStruct((n.rows, n.width), BF16)] * len(sent_steps(n)),
        compiler_params=pltpu.CompilerParams(vmem_limit_bytes=LIMIT),
        cost_estimate=cost(600_000_000),
        name="place_pairs",
    )(*far(*args))


def first_gate_kernel(n, step, dist_ref, atom_ref, feat_ref, *refs):
    sources, held_ref, flipped, left_ref = refs[:6], refs[6], refs[7:13], refs[13]
    for src, dst in zip(sources[:5], flipped[:5]):
        dst[...] = src[...].T
    r = lax.broadcasted_iota(jnp.int32, (n.entries, n.entries), 0)
    q = lax.broadcasted_iota(jnp.int32, (n.entries, n.entries), 1)
    first = whole_div(r, n.orbitals)
    swap = (q == (r - first * n.orbitals) * n.orbitals + first).astype(BF16)
    flipped[5][...] = dot(swap, sources[5][...]).astype(BF16)
    left_ref[...] = dot(flipped[0][...], feat_ref[...], 1, 1).astype(BF16)
    gate = gate_of(dist_ref[:, 0:step], flipped[2][...], flipped[3][...])
    held_ref[...] = gate * dot(left_ref[...], onehot(atom_ref[:, 0:step], n.atoms))


def second_gate_kernel(n, step, dist_ref, atom_ref, left_ref, w_in_ref, w_ro_ref, held_ref):
    gate = gate_of(dist_ref[:, step:], w_in_ref[...], w_ro_ref[...])
    held_ref[...] = gate * dot(left_ref[...], onehot(atom_ref[:, step:], n.atoms))


def first_gate(n, step, distance, pair_atom, features, weights):
    turned = [jax.ShapeDtypeStruct(w.shape[::-1], BF16) for w in weights[:5]]
    turned.append(jax.ShapeDtypeStruct(weights[5].shape, BF16))
    turned.append(jax.ShapeDtypeStruct((n.width, n.atoms), BF16))
    out = pl.pallas_call(
        functools.partial(first_gate_kernel, n, step),
        out_shape=[jax.ShapeDtypeStruct((n.width, step), F32)] + turned,
        compiler_params=pltpu.CompilerParams(vmem_limit_bytes=LIMIT),
        cost_estimate=cost(3_000_000_000),
        name="first_gate",
    )(*far(distance, pair_atom, features, *weights))
    return out[0], out[1:7], out[7]


def second_gate(n, step, distance, pair_atom, left, w_in_t, w_ro_t):
    return pl.pallas_call(
        functools.partial(second_gate_kernel, n, step),
        out_shape=jax.ShapeDtypeStruct((n.width, n.pairs - step), F32),
        compiler_params=pltpu.CompilerParams(vmem_limit_bytes=LIMIT),
        cost_estimate=cost(2_000_000_000),
        name="second_gate",
    )(*far(distance, pair_atom), left, w_in_t, w_ro_t)


def partner_table(n, even, tiles, w_right_t, table_ref):
    right = dot(w_right_t, tiles[0][0 : n.atoms, :], 1, 1).astype(BF16)
    lanes = n.cells * n.part
    k = lax.broadcasted_iota(jnp.int32, (n.fetch, lanes), 0)
    lane = lax.broadcasted_iota(jnp.int32, (n.fetch, lanes), 1)
    m3 = (lane - whole_div(lane, n.part) * n.part) * 3
    mine = lax.broadcasted_iota(jnp.int32, (n.cells, lanes), 0)
    cell = whole_div(lax.broadcasted_iota(jnp.int32, (n.cells, lanes), 1), n.part)
    o_sib = jnp.where(even, 0, 2)
    for role, o in enumerate((1, o_sib, 2 - o_sib)):
        lists = lists_of(n, tiles[role]).astype(BF16)
        per = dot(lists, (k == m3 + o).astype(BF16))
        index = jnp.sum(jnp.where(mine == cell, per, 0.0), 0, keepdims=True)
        table_ref[role] = dot(right, onehot(index.astype(jnp.int32), n.atoms)).astype(BF16)


def received_kernel(n, steps, sections, have, used, first, direct, count, final, *refs):
    held, refs = refs[:count], refs[count:]
    if final:
        calls, extra = final
        mine, refs = refs[:extra], refs[extra:]
    if not first and direct:
        refs = refs[1:]
    outs, refs = refs[: 3 if first else 2], refs[3 if first else 2 :]
    if final:
        (block_ref, own_ref), (rows_buf, own_buf, sem_own, blocks_buf, sem_out) = outs, refs
    else:
        (block_ref, rows_buf), (blocks_buf, sem_out) = outs[:2], refs
    need = held.__getitem__

    me, zi, xi, even = where_am_i()
    o_sib = jnp.where(even, 0, 2)
    roles = (1, o_sib, 2 - o_sib)
    base = len(used)
    near = [(i, at) for i in range(len(steps)) for at in range(n.inner)]
    order = [(role, i, at) for role in have for i, at in near]
    number = {key: g for g, key in enumerate(order)}
    cells = {
        (i, at): jnp.bitwise_xor(zi, steps[i]) * n.inner + jnp.bitwise_xor(xi, at) for i, at in near
    }
    tiles = {
        (u % 3, i, u // 3): need(used.index(u)).at[pl.ds(i * n.rows, n.rows)]
        for u in used
        for i in range(len(steps))
    }
    done = []
    if first:
        own = [tiles[role, 0, 0] for role in range(3)]
        table = outs[2]
        partner_table(n, even, own, need(base + 5)[...], table)
    else:
        table = need(base + 5)
    feats = jnp.concatenate([tiles[key][0 : n.atoms, :] for key in order], 0)
    left = dot(need(base)[...], feats, 1, 1).astype(BF16)

    slabs = []
    for role, i, at in order:
        top = sections[i] * n.section + (role * n.inner + at) * PLANES
        tail = tiles[role, i, at][n.atoms :, 0 : n.slot].astype(F32)
        slabs.append(tail[top : top + PLANES])
    meta = jnp.concatenate(slabs, 1)
    dists = meta[0:1] + meta[1:2] + meta[2:3]
    atoms = meta[3:4].astype(jnp.int32) - 1
    spots = meta[4:5].astype(jnp.int32)

    def cut(x, g):
        return x[:, g * n.slot : (g + 1) * n.slot]

    gate = gate_of(dists, need(base + 1)[...], need(base + 2)[...])
    rights = []
    for role in have:
        place = [cut(spots, number[role, i, at]) + cells[i, at] * n.part for i, at in near]
        rights.append(dot(table[role], onehot(jnp.concatenate(place, 1), n.cells * n.part)))
    lefts = [
        dot(left[:, g * n.atoms : (g + 1) * n.atoms], onehot(cut(atoms, g), n.atoms))
        for g in range(len(order))
    ]
    edge = jnp.concatenate(lefts, 1) * jnp.concatenate(rights, 1) * gate
    mixed = silu(dot(need(base + 3)[...], edge.astype(BF16))).astype(BF16)
    blocks_buf[...] = dot(need(base + 4)[...], mixed).astype(BF16)
    if direct:
        for g, (role, i, at) in enumerate(order):
            place = roles[role] * n.cells + cells[i, at]
            start = pl.multiple_of(place * n.slot, n.slot)
            out = pltpu.make_async_copy(
                blocks_buf.at[:, pl.ds(g * n.slot, n.slot)],
                block_ref.at[:, pl.ds(start, n.slot)],
                sem_out.at[g],
            )
            out.start()
            done.append(out)

    rows = len(order) * n.part
    my_list = lax.broadcasted_iota(jnp.int32, (n.cells, n.fetch), 0) == me
    index = []
    k = lax.broadcasted_iota(jnp.int32, (n.part, n.fetch), 1)
    m3 = 3 * lax.broadcasted_iota(jnp.int32, (n.part, n.fetch), 0)
    asked = {}
    for i, at in near:
        lists = lists_of(n, tiles[0, i, at])
        asked[i, at] = jnp.sum(jnp.where(my_list, lists, 0.0), 0, keepdims=True)
    for g, (role, i, at) in enumerate(order):
        o_own = 1 if role == 0 else 2 - roles[role]
        here = jnp.sum(jnp.where(k == m3 + o_own, asked[i, at], 0.0), 1, keepdims=True)
        index.append(here.astype(jnp.int32) + g * n.atoms)
    lane = lax.broadcasted_iota(jnp.int32, (rows, len(order) * n.atoms), 1)
    pick = (lane == jnp.concatenate(index, 0)).astype(BF16)
    rows_buf[...] = dot(pick, feats).astype(BF16)
    if not direct:
        out = pltpu.make_async_copy(blocks_buf, block_ref, sem_out.at[0])
        out.start()
        done.append(out)
    if final:
        w_mix = need(base + 3)
        done += own_part(n, calls, mine, w_mix, rows_buf, own_buf, own_ref, sem_own, even, zi, xi)
    for out in done:
        out.wait()


def received(n, steps, sections, have, tiles, weights, table, w_right_t, into, own=None):
    first = table is None
    direct = n.slot % 128 == 0
    used = [0, 1, 2, 3, 4, 5] if first else [0, 3] + [3 * at + r for at in (0, 1) for r in have if r]
    if first and 2 not in have:
        used.remove(5)
    used = sorted(set(used))
    operands = [tiles[u] for u in used] + list(weights) + [w_right_t if first else table]
    count = len(operands)
    calls = None
    if own is not None:
        calls, extra = own
        operands += extra
    near = len(operands)
    groups = n.inner * len(have) * len(steps)
    blocks = (n.entries, groups * n.slot)
    rows = (groups * n.part, n.width)
    shape = (3, n.width, n.cells * n.part)
    out_shape = [jax.ShapeDtypeStruct((n.entries, 3 * n.cells * n.slot) if direct else blocks, BF16)]
    scratch = [pltpu.VMEM(blocks, BF16), pltpu.SemaphoreType.DMA((groups,))]
    fast, slow = pl.BlockSpec(memory_space=pltpu.VMEM), pl.BlockSpec(memory_space=pl.ANY)
    if own is not None:
        out_shape.append(jax.ShapeDtypeStruct((n.entries, n.pairs), BF16))
        out_specs = [slow, slow]
        scratch = [
            pltpu.VMEM(rows, BF16),
            pltpu.VMEM((n.entries, n.pairs), BF16),
            pltpu.SemaphoreType.DMA((2,)),
        ] + scratch
    else:
        out_shape.append(jax.ShapeDtypeStruct(rows, BF16))
        out_specs = [slow, fast]
    if first:
        out_shape.append(jax.ShapeDtypeStruct(shape, BF16))
        out_specs.append(fast)
    aliases = {}
    if direct and not first:
        aliases = {near: 0}
        operands.append(into)
    out = pl.pallas_call(
        functools.partial(
            received_kernel, n, steps, sections, have, tuple(used), first, direct, count,
            (calls, near - count) if calls else None,
        ),
        in_specs=[fast] * near + [slow] * (len(operands) - near),
        out_specs=out_specs,
        out_shape=out_shape,
        scratch_shapes=scratch,
        input_output_aliases=aliases,
        compiler_params=pltpu.CompilerParams(vmem_limit_bytes=LIMIT),
        cost_estimate=cost(500_000_000 * groups),
        name="received_blocks",
    )(*operands)
    return out[0], out[1], out[2] if first else table


def own_part(n, calls, mine, w_mix, last, own_buf, own_ref, sem, even, zi, xi):
    row_ref, halves, w_right_ref, w_out_ref, tables = mine[0], mine[1:3], mine[3], mine[4], mine[5:]
    rows = jnp.concatenate([t[...] for t in tables] + [last[...]], 0)
    table = dot(w_right_ref[...], rows, 1, 1).astype(BF16)
    v = row_ref[...]
    q = whole_div(v, n.fetch)
    k = v - q * n.fetch
    m = whole_div(k, 3)
    o = k - 3 * m
    sibling = jnp.where(even, 2, 0)
    role = jnp.where(o == 1, 0, jnp.where(o == sibling, 1, 2))
    outer = whole_div(q, n.inner)
    inner = q - outer * n.inner
    b = jnp.bitwise_xor(outer, zi)
    place, top = b, 0
    for steps, have in calls:
        for r in have:
            for step in steps:
                place = jnp.where((b == step) & (role == r), top, place)
                top += 1
    place = (place * n.inner + jnp.bitwise_xor(inner, xi)) * n.part + m
    done, at = [], 0
    for i, half in enumerate(halves):
        step = half.shape[1]
        right = dot(table, onehot(place[:, at : at + step], table.shape[1]))
        edge = (half[...] * right).astype(BF16)
        mixed = silu(dot(w_mix[...], edge)).astype(BF16)
        own_buf[:, at : at + step] = dot(w_out_ref[...], mixed).astype(BF16)
        part = pl.ds(at, step)
        out = pltpu.make_async_copy(own_buf.at[:, part], own_ref.at[:, part], sem.at[i])
        out.start()
        done.append(out)
        at += step
    return done


def body(
    features,
    pair_atom,
    partner_row,
    transpose_slot,
    distance,
    send_rows,
    w_left,
    w_right,
    w_radial_in,
    w_radial_out,
    w_mix,
    w_out,
):
    n = Sizes(features, pair_atom, send_rows, w_radial_in, w_out)
    lines = n.strips * n.cells

    def exchange(x, partner):
        pairs = []
        for i in range(lines):
            s, c = partner(i // n.cells, i % n.cells)
            pairs.append((i, s * n.cells + c))
        return lax.ppermute(x, AXES, pairs)

    def along(by):
        return lambda s, c: (s, c ^ (by * n.inner))

    def beside(s, c):
        return s, c ^ 1

    def sibling(s, c):
        return s ^ 1, c

    def other(s, c):
        return (s - 1 if s % 2 == 0 else s + 1) % n.strips, c

    row = lambda a: a.reshape(1, -1)
    pair_atom, partner_row = row(pair_atom), row(partner_row)
    transpose_slot, distance = row(transpose_slot), row(distance)
    tiles = make_tiles(
        n, pair_atom, partner_row, transpose_slot, distance, send_rows, features
    )
    lines_in = {0: tiles[0]}
    for b, tile in zip(sent_steps(n), tiles):
        if b:
            lines_in[b] = exchange(tile, along(b))
    for b in range(3, n.outer, 2):
        lines_in[b] = exchange(lines_in[b - 1], along(1))
    step = n.pairs // 2
    held, turned, left = first_gate(
        n,
        step,
        distance,
        pair_atom,
        features,
        (w_left, w_right, w_radial_in, w_radial_out, w_mix, w_out.T),
    )
    second = second_gate(n, step, distance, pair_atom, left, turned[2], turned[3])
    lines_in[1], lines_in[2], second = lax.optimization_barrier((lines_in[1], lines_in[2], second))
    w_left_t, w_right_t, w_in_t, w_ro_t, w_mix_t, w_flip_t = turned
    weights = (w_left_t, w_in_t, w_ro_t, w_mix_t, w_flip_t)
    table, into, tables, parts, calls = None, None, [], [], []

    def take(at, have, table, into, own=None):
        steps, sections, group = sets[at]
        into, rows, table = received(
            n, steps, sections, have, group, weights, table, w_right_t, into, own
        )
        tables.append(rows)
        parts.append(into)
        calls.append((steps, have))
        return table, into

    sets, chain = [], []
    for b in range(0, n.outer, 2):
        tile = jnp.concatenate([lines_in[b], lines_in[b + 1]], 0)
        chain.append([tile, exchange(tile, sibling), exchange(tile, other), exchange(tile, beside)])
        if b:
            before, now = chain[-2], chain[-1]
            before[3], now[1] = lax.optimization_barrier((before[3], now[1]))
    for i, (tile, close, away, across) in enumerate(chain):
        steps, sections = (2 * i, 2 * i + 1), (0, 1 if i else 0)
        if i:
            table, into = take(i - 1, (0, 1), table, into)
        corner = exchange(across, other) if i % 2 else exchange(away, beside)
        group = [tile, close, away, across, exchange(across, sibling), corner]
        sets.append((steps, sections, group))
    last = len(sets) - 1
    table, into = take(last, (0, 1), table, into)
    for i in range(last):
        table, into = take(i, (2,), table, into)
    every = tuple(calls) + ((sets[last][0], (2,)),)
    own = (every, [*far(partner_row), held, second, w_right_t, w_out.T, *tables])
    table, into = take(last, (2,), table, into, own)
    own = tables.pop()
    if n.slot % 128:
        cell, strip = lax.axis_index("cell"), lax.axis_index("strip")
        o_sib = jnp.where(strip % 2 == 0, 0, 2)
        into = jnp.zeros((n.entries, 3 * n.cells * n.slot), BF16)
        for (steps, have), blocks in zip(calls, parts):
            order = [(role, b, at) for role in have for b in steps for at in (0, 1)]
            for g, (role, b, at) in enumerate(order):
                piece = blocks[:, g * n.slot : (g + 1) * n.slot]
                spot = (1, o_sib, 2 - o_sib)[role] * n.cells + (cell ^ (b * n.inner + at))
                into = lax.dynamic_update_slice(into, piece, (0, spot * n.slot))
    return own, into


def solution(mesh):
    split = P(("strip", "cell"))
    wide = P(("strip", "cell"), None)
    in_specs = (wide, split, split, split, split, wide) + (P(),) * 6
    out_specs = (P(None, ("strip", "cell")), P(None, ("strip", "cell")))
    return jax.shard_map(body, mesh=mesh, in_specs=in_specs, out_specs=out_specs, check_vma=False)
```

```python
import functools

import jax
import jax.numpy as jnp
from jax import lax
from jax.experimental import pallas as pl
from jax.experimental.pallas import tpu as pltpu
from jax.sharding import PartitionSpec as P

cutoff = 8.0
PLANES = 5
LIST = 64
LIMIT = 36 << 20
BF16 = jnp.bfloat16
F32 = jnp.float32
AXES = ("strip", "cell")


def up(n, by):
    return -(-n // by) * by


def whole_div(x, by):
    return jnp.floor((x.astype(F32) + 0.5) * (1.0 / by)).astype(jnp.int32)


def dot(a, b, ca=1, cb=0):
    return lax.dot_general(a, b, (((ca,), (cb,)), ((), ())), preferred_element_type=F32)


def silu(x):
    half = 0.5 * x
    return half + half * jnp.tanh(half)


def onehot(index, count):
    rows = lax.broadcasted_iota(jnp.int32, (count, index.shape[1]), 0)
    return (rows == index).astype(BF16)


def gate_of(distance, w_in_t, w_out_t):
    count = w_in_t.shape[1]
    centers = lax.broadcasted_iota(jnp.int32, (count, 1), 0).astype(F32) * (cutoff / (count - 1))
    scaled = (distance - centers) * (count / (2.0 * cutoff))
    envelope = 0.5 * (jnp.cos(distance * (jnp.pi / cutoff)) + 1.0)
    basis = (jnp.exp(-scaled * scaled) * envelope).astype(BF16)
    radial = silu(dot(w_in_t, basis)).astype(BF16)
    return dot(w_out_t, radial)


def whole(a):
    return pl.BlockSpec(a.shape, lambda *_: (0,) * a.ndim)


def far(*arrays):
    return [pltpu.with_memory_space_constraint(a, pltpu.HBM) for a in arrays]


def cost(flops, nbytes=1 << 20):
    return pl.CostEstimate(flops=flops, bytes_accessed=nbytes, transcendentals=0)


class Sizes:
    def __init__(self, features, pair_atom, send_rows, w_radial_in, w_out):
        self.atoms, self.width = features.shape
        self.pairs = pair_atom.shape[0]
        self.cells, self.fetch = send_rows.shape
        self.strips = lax.axis_size("strip")
        self.inner = 2
        self.outer = self.cells // 2
        self.slot = self.pairs // (2 * self.cells)
        self.part = self.fetch // 3
        self.groups = 3 * self.inner
        self.meta = PLANES * self.groups
        self.per_row = self.width // LIST
        self.tail = up(self.meta + -(-self.cells // self.per_row), 16)
        self.rows = self.atoms + self.tail
        self.entries = w_out.shape[1]
        self.orbitals = int(self.entries**0.5 + 0.5)


def where_am_i():
    strip, cell = lax.axis_index("strip"), lax.axis_index("cell")
    even = lax.rem(strip, 2) == 0
    return cell, lax.div(cell, 2), lax.rem(cell, 2), even


def sent_steps(n):
    return [b for b in range(n.outer) if b < 2 or b % 2 == 0]


def tiles_kernel(n, atom_ref, row_ref, slot_ref, dist_ref, list_ref, feat_ref, *outs):
    _, zi, xi, even = where_am_i()
    slot = slot_ref[...]
    hi = whole_div(slot, n.slot)
    lo = slot - hi * n.slot
    row = row_ref[...]
    k = row - whole_div(row, n.fetch) * n.fetch
    dist = dist_ref[...]
    d1 = dist.astype(BF16)
    rest = dist - d1.astype(F32)
    d2 = rest.astype(BF16)
    d3 = (rest - d2.astype(F32)).astype(BF16)
    planes = [
        d1.astype(F32),
        d2.astype(F32),
        d3.astype(F32),
        (atom_ref[...] + 1).astype(F32),
        whole_div(k, 3).astype(F32),
    ]
    total = 3 * n.cells
    mask = lax.broadcasted_iota(jnp.int32, (total, n.pairs), 0) == hi
    spread = jnp.concatenate([jnp.where(mask, p, 0.0) for p in planes], 0).astype(BF16)
    placed = dot(spread, onehot(lo, n.slot), 1, 1).astype(BF16)
    shape = (n.tail, PLANES * total)
    r = lax.broadcasted_iota(jnp.int32, shape, 0)
    q = lax.broadcasted_iota(jnp.int32, shape, 1)
    g = whole_div(r, PLANES)
    plane = r - g * PLANES
    role = whole_div(g, n.inner)
    o = jnp.where(role == 0, 1, jnp.where((role == 1) == even, 2, 0))
    base = plane * total + o * n.cells + jnp.bitwise_xor(g - role * n.inner, xi)
    base = jnp.where(r < n.meta, base, -n.pairs)
    e = list_ref[...]
    kk = lax.broadcasted_iota(jnp.int32, e.shape, 1)
    e = (e - (kk - whole_div(kk, 3) * 3) * n.atoms).astype(F32)
    wide = jnp.concatenate([e, jnp.zeros((n.cells, LIST - n.fetch), F32)], 1)
    flat = jnp.concatenate([wide] * n.per_row, 1)
    j = lax.broadcasted_iota(jnp.int32, flat.shape, 0)
    lane = lax.broadcasted_iota(jnp.int32, flat.shape, 1)
    at_row = whole_div(j, n.per_row)
    flat = jnp.where(whole_div(lane, LIST) == j - at_row * n.per_row, flat, 0.0).astype(BF16)
    put_r = lax.broadcasted_iota(jnp.int32, (n.tail, n.cells), 0)
    put_j = lax.broadcasted_iota(jnp.int32, (n.tail, n.cells), 1)
    put = (put_r == n.meta + whole_div(put_j, n.per_row)).astype(BF16)
    lists = dot(put, flat)
    feat = feat_ref[...]

    def tail(b):
        pick = (base + jnp.bitwise_xor(zi, b) * n.inner == q).astype(BF16)
        pairs = dot(pick, placed)
        if n.slot < n.width:
            pairs = jnp.concatenate([pairs, jnp.zeros((n.tail, n.width - n.slot), F32)], 1)
        return (pairs + lists).astype(BF16)

    for b, out in zip(sent_steps(n), outs):
        top = 0
        if b > 1:
            out[0 : n.tail, :] = tail(b + 1)
            top = n.tail
        out[top : top + n.atoms, :] = feat
        out[top + n.atoms :, :] = tail(b)


def lists_of(n, tail):
    tail = tail.astype(F32)
    rows = []
    for j in range(n.cells):
        r = n.meta + j // n.per_row
        lane = LIST * (j % n.per_row)
        rows.append(tail[r : r + 1, lane : lane + n.fetch])
    return jnp.concatenate(rows, 0)


def make_tiles(n, pair_atom, partner_row, transpose_slot, distance, send_rows, features):
    args = (pair_atom, partner_row, transpose_slot, distance, send_rows, features)
    return pl.pallas_call(
        functools.partial(tiles_kernel, n),
        out_shape=[
            jax.ShapeDtypeStruct((n.rows + (n.tail if b > 1 else 0), n.width), BF16)
            for b in sent_steps(n)
        ],
        compiler_params=pltpu.CompilerParams(vmem_limit_bytes=LIMIT),
        cost_estimate=cost(600_000_000),
        name="place_pairs",
    )(*far(*args))


def first_gate_kernel(n, step, dist_ref, atom_ref, feat_ref, *refs):
    sources, held_ref, flipped, left_ref = refs[:6], refs[6], refs[7:13], refs[13]
    for src, dst in zip(sources[:5], flipped[:5]):
        dst[...] = src[...].T
    r = lax.broadcasted_iota(jnp.int32, (n.entries, n.entries), 0)
    q = lax.broadcasted_iota(jnp.int32, (n.entries, n.entries), 1)
    first = whole_div(r, n.orbitals)
    swap = (q == (r - first * n.orbitals) * n.orbitals + first).astype(BF16)
    flipped[5][...] = dot(swap, sources[5][...]).astype(BF16)
    left_ref[...] = dot(flipped[0][...], feat_ref[...], 1, 1).astype(BF16)
    gate = gate_of(dist_ref[:, 0:step], flipped[2][...], flipped[3][...])
    held_ref[...] = gate * dot(left_ref[...], onehot(atom_ref[:, 0:step], n.atoms))


def second_gate_kernel(n, step, dist_ref, atom_ref, left_ref, w_in_ref, w_ro_ref, held_ref):
    gate = gate_of(dist_ref[:, step:], w_in_ref[...], w_ro_ref[...])
    held_ref[...] = gate * dot(left_ref[...], onehot(atom_ref[:, step:], n.atoms))


def first_gate(n, step, distance, pair_atom, features, weights):
    turned = [jax.ShapeDtypeStruct(w.shape[::-1], BF16) for w in weights[:5]]
    turned.append(jax.ShapeDtypeStruct(weights[5].shape, BF16))
    turned.append(jax.ShapeDtypeStruct((n.width, n.atoms), BF16))
    out = pl.pallas_call(
        functools.partial(first_gate_kernel, n, step),
        out_shape=[jax.ShapeDtypeStruct((n.width, step), F32)] + turned,
        compiler_params=pltpu.CompilerParams(vmem_limit_bytes=LIMIT),
        cost_estimate=cost(3_000_000_000),
        name="first_gate",
    )(*far(distance, pair_atom, features, *weights))
    return out[0], out[1:7], out[7]


def second_gate(n, step, distance, pair_atom, left, w_in_t, w_ro_t):
    return pl.pallas_call(
        functools.partial(second_gate_kernel, n, step),
        out_shape=jax.ShapeDtypeStruct((n.width, n.pairs - step), F32),
        compiler_params=pltpu.CompilerParams(vmem_limit_bytes=LIMIT),
        cost_estimate=cost(2_000_000_000),
        name="second_gate",
    )(*far(distance, pair_atom), left, w_in_t, w_ro_t)


def partner_table(n, even, feat, tails, w_right_t, table_ref):
    right = dot(w_right_t, feat, 1, 1).astype(BF16)
    lanes = n.cells * n.part
    k = lax.broadcasted_iota(jnp.int32, (n.fetch, lanes), 0)
    lane = lax.broadcasted_iota(jnp.int32, (n.fetch, lanes), 1)
    m3 = (lane - whole_div(lane, n.part) * n.part) * 3
    mine = lax.broadcasted_iota(jnp.int32, (n.cells, lanes), 0)
    cell = whole_div(lax.broadcasted_iota(jnp.int32, (n.cells, lanes), 1), n.part)
    o_sib = jnp.where(even, 0, 2)
    for role, o in enumerate((1, o_sib, 2 - o_sib)):
        lists = lists_of(n, tails[role]).astype(BF16)
        per = dot(lists, (k == m3 + o).astype(BF16))
        index = jnp.sum(jnp.where(mine == cell, per, 0.0), 0, keepdims=True)
        table_ref[role] = dot(right, onehot(index.astype(jnp.int32), n.atoms)).astype(BF16)


def received_kernel(n, steps, have, used, first, direct, count, final, *refs):
    held, refs = refs[:count], refs[count:]
    if final:
        calls, extra, old = final
        mine, refs = refs[:extra], refs[extra:]
    if final:
        earlier, mine = mine[:old], mine[old:]
        block_ref, own_ref, rows_buf, own_buf, sem_own, blocks_buf, sem_out = refs
    else:
        blocks_buf, rows_buf = refs[:2]
    need = held.__getitem__
    need = held.__getitem__

    me, zi, xi, even = where_am_i()
    o_sib = jnp.where(even, 0, 2)
    roles = (1, o_sib, 2 - o_sib)
    base = len(used)
    near = [(i, at) for i in range(len(steps)) for at in range(n.inner)]
    order = [(role, i, at) for role, at in have for i in range(len(steps))]
    number = {key: g for g, key in enumerate(order)}
    cells = {
        (i, at): jnp.bitwise_xor(zi, steps[i]) * n.inner + jnp.bitwise_xor(xi, at) for i, at in near
    }
    u_at = {u: j for j, u in enumerate(used)}
    feat_of, tail_of = {}, {}
    for u in used:
        for i, b in enumerate(steps):
            tail_first = b > 1 and b % 2 == 1
            top, end = i * n.rows, (i + 1) * n.rows
            cut_at = top + (n.tail if tail_first else n.atoms)
            parts = need(u_at[u]).at[pl.ds(top, cut_at - top)], need(u_at[u]).at[pl.ds(cut_at, end - cut_at)]
            tail_of[u % 3, i, u // 3], feat_of[u % 3, i, u // 3] = parts if tail_first else parts[::-1]
    done = []

    def put(buf, at, order):
        for g, (role, b, beside) in enumerate(order):
            cell = jnp.bitwise_xor(zi, b) * n.inner + jnp.bitwise_xor(xi, beside)
            start = pl.multiple_of((roles[role] * n.cells + cell) * n.slot, n.slot)
            out = pltpu.make_async_copy(
                buf.at[:, pl.ds(g * n.slot, n.slot)],
                block_ref.at[:, pl.ds(start, n.slot)],
                sem_out.at[at + g],
            )
            out.start()
            done.append(out)

    if final and direct:
        sent = len(order)
        for buf, (planes, kinds) in zip(earlier, calls):
            spots = [(role, b, beside) for role, beside in kinds for b in planes]
            put(buf, sent, spots)
            sent += len(spots)
    if first:
        tails = [tail_of[role, 0, 0][...] for role in range(3)]
        table = refs[2]
        partner_table(n, even, feat_of[0, 0, 0][...], tails, need(base + 5)[...], table)
    else:
        table = need(base + 5)
    feats = jnp.concatenate([feat_of[key][...] for key in order], 0)
    left = dot(need(base)[...], feats, 1, 1).astype(BF16)

    slabs = []
    for role, i, at in order:
        top = (role * n.inner + at) * PLANES
        tail = tail_of[role, i, at][:, 0 : n.slot].astype(F32)
        slabs.append(tail[top : top + PLANES])
    meta = jnp.concatenate(slabs, 1)
    dists = meta[0:1] + meta[1:2] + meta[2:3]
    atoms = meta[3:4].astype(jnp.int32) - 1
    spots = meta[4:5].astype(jnp.int32)

    def cut(x, g):
        return x[:, g * n.slot : (g + 1) * n.slot]

    gate = gate_of(dists, need(base + 1)[...], need(base + 2)[...])
    rights = []
    for role in sorted({role for role, _ in have}):
        asking = [key for key in order if key[0] == role]
        place = [cut(spots, number[key]) + cells[key[1:]] * n.part for key in asking]
        rights.append(dot(table[role], onehot(jnp.concatenate(place, 1), n.cells * n.part)))
    lefts = [
        dot(left[:, g * n.atoms : (g + 1) * n.atoms], onehot(cut(atoms, g), n.atoms))
        for g in range(len(order))
    ]
    edge = jnp.concatenate(lefts, 1) * jnp.concatenate(rights, 1) * gate
    mixed = silu(dot(need(base + 3)[...], edge.astype(BF16))).astype(BF16)
    blocks_buf[...] = dot(need(base + 4)[...], mixed).astype(BF16)
    if final and direct:
        put(blocks_buf, 0, [(role, steps[i], at) for role, i, at in order])

    rows = len(order) * n.part
    my_list = lax.broadcasted_iota(jnp.int32, (n.cells, n.fetch), 0) == me
    index = []
    k = lax.broadcasted_iota(jnp.int32, (n.part, n.fetch), 1)
    m3 = 3 * lax.broadcasted_iota(jnp.int32, (n.part, n.fetch), 0)
    asked = {}
    for i, at in sorted({key[1:] for key in order}):
        lists = lists_of(n, tail_of[0, i, at][...])
        asked[i, at] = jnp.sum(jnp.where(my_list, lists, 0.0), 0, keepdims=True)
    for g, (role, i, at) in enumerate(order):
        o_own = 1 if role == 0 else 2 - roles[role]
        here = jnp.sum(jnp.where(k == m3 + o_own, asked[i, at], 0.0), 1, keepdims=True)
        index.append(here.astype(jnp.int32) + g * n.atoms)
    lane = lax.broadcasted_iota(jnp.int32, (rows, len(order) * n.atoms), 1)
    pick = (lane == jnp.concatenate(index, 0)).astype(BF16)
    rows_buf[...] = dot(pick, feats).astype(BF16)
    if final and not direct:
        out = pltpu.make_async_copy(blocks_buf, block_ref, sem_out.at[0])
        out.start()
        done.append(out)
    if final:
        w_mix = need(base + 3)
        done += own_part(n, calls, mine, w_mix, rows_buf, own_buf, own_ref, sem_own, even, zi, xi)
    for out in done:
        out.wait()


def received(n, steps, have, tiles, weights, table, w_right_t, own=None):
    first = table is None
    direct = n.slot % 128 == 0
    used = {u for role, at in have for u in (3 * at, 3 * at + role)}
    used = sorted(used | ({0, 1, 2} if first else set()))
    operands = [tiles[u] for u in used] + list(weights) + [w_right_t if first else table]
    count = len(operands)
    groups = len(have) * len(steps)
    blocks = (n.entries, groups * n.slot)
    rows = (groups * n.part, n.width)
    fast, slow = pl.BlockSpec(memory_space=pltpu.VMEM), pl.BlockSpec(memory_space=pl.ANY)
    final, scratch = None, []
    if own is None:
        out_shape = [jax.ShapeDtypeStruct(blocks, BF16), jax.ShapeDtypeStruct(rows, BF16)]
        out_specs = [fast, fast]
        if first:
            shape = (3, n.width, n.cells * n.part)
            out_shape.append(jax.ShapeDtypeStruct(shape, BF16))
            out_specs.append(fast)
    else:
        calls, earlier, extra = own
        total = 3 * n.cells
        operands += [*earlier, *extra]
        final = calls, len(operands) - count, len(earlier)
        shape = (n.entries, total * n.slot) if direct else blocks
        out_shape = [
            jax.ShapeDtypeStruct(shape, BF16),
            jax.ShapeDtypeStruct((n.entries, n.pairs), BF16),
        ]
        out_specs = [slow, slow]
        scratch = [
            pltpu.VMEM(rows, BF16),
            pltpu.VMEM((n.entries, n.pairs), BF16),
            pltpu.SemaphoreType.DMA((2,)),
            pltpu.VMEM(blocks, BF16),
            pltpu.SemaphoreType.DMA((total if direct else 1,)),
        ]
    return pl.pallas_call(
        functools.partial(received_kernel, n, steps, have, tuple(used), first, direct, count, final),
        in_specs=[fast] * len(operands),
        out_specs=out_specs,
        out_shape=out_shape,
        scratch_shapes=scratch,
        compiler_params=pltpu.CompilerParams(vmem_limit_bytes=LIMIT),
        cost_estimate=cost(500_000_000 * groups),
        name="received_blocks",
    )(*operands)


def own_part(n, calls, mine, w_mix, last, own_buf, own_ref, sem, even, zi, xi):
    row_ref, halves, w_right_ref, w_out_ref, tables = mine[0], mine[1:3], mine[3], mine[4], mine[5:]
    rows = jnp.concatenate([t[...] for t in tables] + [last[...]], 0)
    table = dot(w_right_ref[...], rows, 1, 1).astype(BF16)
    v = row_ref[...]
    q = whole_div(v, n.fetch)
    k = v - q * n.fetch
    m = whole_div(k, 3)
    o = k - 3 * m
    sibling = jnp.where(even, 2, 0)
    role = jnp.where(o == 1, 0, jnp.where(o == sibling, 1, 2))
    outer = whole_div(q, n.inner)
    inner = q - outer * n.inner
    b = jnp.bitwise_xor(outer, zi)
    place, top = b, 0
    for steps, have in calls:
        for r, beside in have:
            for step in steps:
                here = (b == step) & (role == r) & (jnp.bitwise_xor(inner, xi) == beside)
                place = jnp.where(here, top, place)
                top += 1
    place = place * n.part + m
    done, at = [], 0
    for i, half in enumerate(halves):
        step = half.shape[1]
        right = dot(table, onehot(place[:, at : at + step], table.shape[1]))
        edge = (half[...] * right).astype(BF16)
        mixed = silu(dot(w_mix[...], edge)).astype(BF16)
        own_buf[:, at : at + step] = dot(w_out_ref[...], mixed).astype(BF16)
        part = pl.ds(at, step)
        out = pltpu.make_async_copy(own_buf.at[:, part], own_ref.at[:, part], sem.at[i])
        out.start()
        done.append(out)
        at += step
    return done


def body(
    features,
    pair_atom,
    partner_row,
    transpose_slot,
    distance,
    send_rows,
    w_left,
    w_right,
    w_radial_in,
    w_radial_out,
    w_mix,
    w_out,
):
    n = Sizes(features, pair_atom, send_rows, w_radial_in, w_out)
    lines = n.strips * n.cells

    def exchange(x, partner):
        pairs = []
        for i in range(lines):
            s, c = partner(i // n.cells, i % n.cells)
            pairs.append((i, s * n.cells + c))
        return lax.ppermute(x, AXES, pairs)

    def along(by):
        return lambda s, c: (s, c ^ (by * n.inner))

    def beside(s, c):
        return s, c ^ 1

    def sibling(s, c):
        return s ^ 1, c

    def other(s, c):
        return (s - 1 if s % 2 == 0 else s + 1) % n.strips, c

    row = lambda a: a.reshape(1, -1)
    pair_atom, partner_row = row(pair_atom), row(partner_row)
    transpose_slot, distance = row(transpose_slot), row(distance)
    tiles = make_tiles(
        n, pair_atom, partner_row, transpose_slot, distance, send_rows, features
    )
    lines_in = {0: tiles[0]}
    for b, tile in zip(sent_steps(n), tiles):
        if b:
            lines_in[b] = exchange(tile, along(b))
    for b in range(3, n.outer, 2):
        lines_in[b] = exchange(lines_in[b - 1], along(1))
    step = n.pairs // 2
    held, turned, left = first_gate(
        n,
        step,
        distance,
        pair_atom,
        features,
        (w_left, w_right, w_radial_in, w_radial_out, w_mix, w_out.T),
    )
    second = second_gate(n, step, distance, pair_atom, left, turned[2], turned[3])
    lines_in[1], lines_in[2], second = lax.optimization_barrier((lines_in[1], lines_in[2], second))
    w_left_t, w_right_t, w_in_t, w_ro_t, w_mix_t, w_flip_t = turned
    weights = (w_left_t, w_in_t, w_ro_t, w_mix_t, w_flip_t)
    tables, parts, calls = [], [], []

    def take(at, have, table):
        steps, group = sets[at]
        blocks, rows, *new = received(n, steps, have, group, weights, table, w_right_t)
        tables.append(rows)
        parts.append(blocks)
        calls.append((steps, have))
        return new[0] if new else table

    sets, chain = [], []
    for b in range(0, n.outer, 2):
        tile = jnp.concatenate([lines_in[b][-n.rows :], lines_in[b + 1][: n.rows]], 0)
        chain.append([tile, exchange(tile, sibling), exchange(tile, other), exchange(tile, beside)])
    for i, (tile, close, away, across) in enumerate(chain):
        corner_tile = exchange(across, other) if i % 2 else exchange(away, beside)
        group = [tile, close, away, across, exchange(across, sibling), corner_tile]
        sets.append(((2 * i, 2 * i + 1), group))
    last, table = len(sets) - 1, None
    same_strips, away_near, away_far = ((0, 0), (0, 1), (1, 0), (1, 1)), ((2, 0),), ((2, 1),)
    for i in range(last + 1):
        table = take(i, same_strips, table)
    for i in range(last):
        table = take(i, away_near + away_far, table)
    table = take(last, away_near, table)
    every = (*calls, (sets[last][0], away_far))
    earlier = parts if n.slot % 128 == 0 else []
    own = (every, earlier, [*far(partner_row), held, second, w_right_t, w_out.T, *tables])
    into, own = received(n, sets[last][0], away_far, sets[last][1], weights, table, w_right_t, own)
    if n.slot % 128:
        cell, strip = lax.axis_index("cell"), lax.axis_index("strip")
        o_sib = jnp.where(strip % 2 == 0, 0, 2)
        parts.append(into)
        into = jnp.zeros((n.entries, 3 * n.cells * n.slot), BF16)
        for (steps, have), blocks in zip(every, parts):
            order = [(role, b, at) for role, at in have for b in steps]
            for g, (role, b, at) in enumerate(order):
                piece = blocks[:, g * n.slot : (g + 1) * n.slot]
                spot = (1, o_sib, 2 - o_sib)[role] * n.cells + (cell ^ (b * n.inner + at))
                into = lax.dynamic_update_slice(into, piece, (0, spot * n.slot))
    return own, into


def solution(mesh):
    split = P(("strip", "cell"))
    wide = P(("strip", "cell"), None)
    in_specs = (wide, split, split, split, split, wide) + (P(),) * 6
    out_specs = (P(None, ("strip", "cell")), P(None, ("strip", "cell")))
    return jax.shard_map(body, mesh=mesh, in_specs=in_specs, out_specs=out_specs, check_vma=False)
```

```python
import functools

import jax
import jax.numpy as jnp
from jax import lax
from jax.experimental import pallas as pl
from jax.experimental.pallas import tpu as pltpu
from jax.sharding import PartitionSpec as P

cutoff = 8.0
PLANES = 5
LIST = 64
LIMIT = 36 << 20
BF16 = jnp.bfloat16
F32 = jnp.float32
AXES = ("strip", "cell")


def up(n, by):
    return -(-n // by) * by


def whole_div(x, by):
    return jnp.floor((x.astype(F32) + 0.5) * (1.0 / by)).astype(jnp.int32)


def dot(a, b, ca=1, cb=0):
    return lax.dot_general(a, b, (((ca,), (cb,)), ((), ())), preferred_element_type=F32)


def silu(x):
    half = 0.5 * x
    return half + half * jnp.tanh(half)


def onehot(index, count):
    rows = lax.broadcasted_iota(jnp.int32, (count, index.shape[1]), 0)
    return (rows == index).astype(BF16)


def gate_of(distance, w_in_t, w_out_t):
    count = w_in_t.shape[1]
    centers = lax.broadcasted_iota(jnp.int32, (count, 1), 0).astype(F32) * (cutoff / (count - 1))
    scaled = (distance - centers) * (count / (2.0 * cutoff))
    envelope = 0.5 * (jnp.cos(distance * (jnp.pi / cutoff)) + 1.0)
    basis = (jnp.exp(-scaled * scaled) * envelope).astype(BF16)
    radial = silu(dot(w_in_t, basis)).astype(BF16)
    return dot(w_out_t, radial)


def whole(a):
    return pl.BlockSpec(a.shape, lambda *_: (0,) * a.ndim)


def far(*arrays):
    return [pltpu.with_memory_space_constraint(a, pltpu.HBM) for a in arrays]


def cost(flops, nbytes=1 << 20):
    return pl.CostEstimate(flops=flops, bytes_accessed=nbytes, transcendentals=0)


class Sizes:
    def __init__(self, features, pair_atom, send_rows, w_radial_in, w_out):
        self.atoms, self.width = features.shape
        self.pairs = pair_atom.shape[0]
        self.cells, self.fetch = send_rows.shape
        self.strips = lax.axis_size("strip")
        self.inner = 2
        self.outer = self.cells // 2
        self.slot = self.pairs // (2 * self.cells)
        self.part = self.fetch // 3
        self.groups = 3 * self.inner
        self.meta = PLANES * self.groups
        self.per_row = self.width // LIST
        self.tail = up(self.meta + -(-self.cells // self.per_row), 16)
        self.rows = self.atoms + self.tail
        self.entries = w_out.shape[1]
        self.orbitals = int(self.entries**0.5 + 0.5)


def where_am_i():
    strip, cell = lax.axis_index("strip"), lax.axis_index("cell")
    even = lax.rem(strip, 2) == 0
    return cell, lax.div(cell, 2), lax.rem(cell, 2), even


def sent_steps(n):
    return [b for b in range(n.outer) if b < 2 or b % 2 == 0]


def tiles_kernel(n, atom_ref, row_ref, slot_ref, dist_ref, list_ref, feat_ref, *outs):
    _, zi, xi, even = where_am_i()
    slot = slot_ref[...]
    hi = whole_div(slot, n.slot)
    lo = slot - hi * n.slot
    row = row_ref[...]
    k = row - whole_div(row, n.fetch) * n.fetch
    dist = dist_ref[...]
    d1 = dist.astype(BF16)
    rest = dist - d1.astype(F32)
    d2 = rest.astype(BF16)
    d3 = (rest - d2.astype(F32)).astype(BF16)
    planes = [
        d1.astype(F32),
        d2.astype(F32),
        d3.astype(F32),
        (atom_ref[...] + 1).astype(F32),
        whole_div(k, 3).astype(F32),
    ]
    total = 3 * n.cells
    mask = lax.broadcasted_iota(jnp.int32, (total, n.pairs), 0) == hi
    spread = jnp.concatenate([jnp.where(mask, p, 0.0) for p in planes], 0).astype(BF16)
    placed = dot(spread, onehot(lo, n.slot), 1, 1).astype(BF16)
    shape = (n.tail, PLANES * total)
    r = lax.broadcasted_iota(jnp.int32, shape, 0)
    q = lax.broadcasted_iota(jnp.int32, shape, 1)
    g = whole_div(r, PLANES)
    plane = r - g * PLANES
    role = whole_div(g, n.inner)
    o = jnp.where(role == 0, 1, jnp.where((role == 1) == even, 2, 0))
    base = plane * total + o * n.cells + jnp.bitwise_xor(g - role * n.inner, xi)
    base = jnp.where(r < n.meta, base, -n.pairs)
    e = list_ref[...]
    kk = lax.broadcasted_iota(jnp.int32, e.shape, 1)
    e = (e - (kk - whole_div(kk, 3) * 3) * n.atoms).astype(F32)
    wide = jnp.concatenate([e, jnp.zeros((n.cells, LIST - n.fetch), F32)], 1)
    flat = jnp.concatenate([wide] * n.per_row, 1)
    j = lax.broadcasted_iota(jnp.int32, flat.shape, 0)
    lane = lax.broadcasted_iota(jnp.int32, flat.shape, 1)
    at_row = whole_div(j, n.per_row)
    flat = jnp.where(whole_div(lane, LIST) == j - at_row * n.per_row, flat, 0.0).astype(BF16)
    put_r = lax.broadcasted_iota(jnp.int32, (n.tail, n.cells), 0)
    put_j = lax.broadcasted_iota(jnp.int32, (n.tail, n.cells), 1)
    put = (put_r == n.meta + whole_div(put_j, n.per_row)).astype(BF16)
    lists = dot(put, flat)
    feat = feat_ref[...]

    def tail(b):
        pick = (base + jnp.bitwise_xor(zi, b) * n.inner == q).astype(BF16)
        pairs = dot(pick, placed)
        if n.slot < n.width:
            pairs = jnp.concatenate([pairs, jnp.zeros((n.tail, n.width - n.slot), F32)], 1)
        return (pairs + lists).astype(BF16)

    for b, out in zip(sent_steps(n), outs):
        top = 0
        if b > 1:
            out[0 : n.tail, :] = tail(b + 1)
            top = n.tail
        out[top : top + n.atoms, :] = feat
        out[top + n.atoms :, :] = tail(b)


def lists_of(n, tail):
    tail = tail.astype(F32)
    rows = []
    for j in range(n.cells):
        r = n.meta + j // n.per_row
        lane = LIST * (j % n.per_row)
        rows.append(tail[r : r + 1, lane : lane + n.fetch])
    return jnp.concatenate(rows, 0)


def make_tiles(n, pair_atom, partner_row, transpose_slot, distance, send_rows, features):
    args = (pair_atom, partner_row, transpose_slot, distance, send_rows, features)
    return pl.pallas_call(
        functools.partial(tiles_kernel, n),
        out_shape=[
            jax.ShapeDtypeStruct((n.rows + (n.tail if b > 1 else 0), n.width), BF16)
            for b in sent_steps(n)
        ],
        compiler_params=pltpu.CompilerParams(vmem_limit_bytes=LIMIT),
        cost_estimate=cost(600_000_000),
        name="place_pairs",
    )(*far(*args))


def first_gate_kernel(n, step, dist_ref, atom_ref, feat_ref, *refs):
    sources, held_ref, flipped, left_ref = refs[:6], refs[6], refs[7:13], refs[13]
    refs[14][...] = sources[5][...]
    for src, dst in zip(sources[:5], flipped[:5]):
        dst[...] = src[...].T
    r = lax.broadcasted_iota(jnp.int32, (n.entries, n.entries), 0)
    q = lax.broadcasted_iota(jnp.int32, (n.entries, n.entries), 1)
    first = whole_div(r, n.orbitals)
    swap = (q == (r - first * n.orbitals) * n.orbitals + first).astype(BF16)
    flipped[5][...] = dot(swap, sources[5][...]).astype(BF16)
    left_ref[...] = dot(flipped[0][...], feat_ref[...], 1, 1).astype(BF16)
    gate = gate_of(dist_ref[:, 0:step], flipped[2][...], flipped[3][...])
    held_ref[...] = gate * dot(left_ref[...], onehot(atom_ref[:, 0:step], n.atoms))


def second_gate_kernel(n, step, dist_ref, atom_ref, row_ref, left_ref, w_in_ref, w_ro_ref, *outs):
    held_ref, place_ref = outs
    gate = gate_of(dist_ref[:, step:], w_in_ref[...], w_ro_ref[...])
    held_ref[...] = gate * dot(left_ref[...], onehot(atom_ref[:, step:], n.atoms))
    _, zi, xi, even = where_am_i()
    v = row_ref[...]
    q = whole_div(v, n.fetch)
    k = v - q * n.fetch
    m = whole_div(k, 3)
    o = k - 3 * m
    sibling = jnp.where(even, 2, 0)
    role = jnp.where(o == 1, 0, jnp.where(o == sibling, 1, 2))
    outer = whole_div(q, n.inner)
    beside = jnp.bitwise_xor(q - outer * n.inner, xi)
    b = jnp.bitwise_xor(outer, zi)
    place_ref[...] = ((b * 3 + role) * n.inner + beside) * n.part + m


def first_gate(n, step, distance, pair_atom, features, weights):
    turned = [jax.ShapeDtypeStruct(w.shape[::-1], BF16) for w in weights[:5]]
    turned.append(jax.ShapeDtypeStruct(weights[5].shape, BF16))
    turned.append(jax.ShapeDtypeStruct((n.width, n.atoms), BF16))
    turned.append(jax.ShapeDtypeStruct(weights[5].shape, BF16))
    out = pl.pallas_call(
        functools.partial(first_gate_kernel, n, step),
        out_shape=[jax.ShapeDtypeStruct((n.width, step), F32)] + turned,
        compiler_params=pltpu.CompilerParams(vmem_limit_bytes=LIMIT),
        cost_estimate=cost(3_000_000_000),
        name="first_gate",
    )(*far(distance, pair_atom, features, *weights))
    return out[0], out[1:7], out[7], out[8]


def second_gate(n, step, distance, pair_atom, partner_row, left, w_in_t, w_ro_t):
    return pl.pallas_call(
        functools.partial(second_gate_kernel, n, step),
        out_shape=[
            jax.ShapeDtypeStruct((n.width, n.pairs - step), F32),
            jax.ShapeDtypeStruct((1, n.pairs), jnp.int32),
        ],
        compiler_params=pltpu.CompilerParams(vmem_limit_bytes=LIMIT),
        cost_estimate=cost(2_000_000_000),
        name="second_gate",
    )(*far(distance, pair_atom, partner_row), left, w_in_t, w_ro_t)


def partner_table(n, even, feat, tails, w_right_t, table_ref):
    right = dot(w_right_t, feat, 1, 1).astype(BF16)
    lanes = n.cells * n.part
    k = lax.broadcasted_iota(jnp.int32, (n.fetch, lanes), 0)
    lane = lax.broadcasted_iota(jnp.int32, (n.fetch, lanes), 1)
    m3 = (lane - whole_div(lane, n.part) * n.part) * 3
    mine = lax.broadcasted_iota(jnp.int32, (n.cells, lanes), 0)
    cell = whole_div(lax.broadcasted_iota(jnp.int32, (n.cells, lanes), 1), n.part)
    o_sib = jnp.where(even, 0, 2)
    for role, o in enumerate((1, o_sib, 2 - o_sib)):
        lists = lists_of(n, tails[role]).astype(BF16)
        per = dot(lists, (k == m3 + o).astype(BF16))
        index = jnp.sum(jnp.where(mine == cell, per, 0.0), 0, keepdims=True)
        table_ref[role] = dot(right, onehot(index.astype(jnp.int32), n.atoms)).astype(BF16)


def received_kernel(n, steps, have, used, first, direct, count, final, *refs):
    held, refs = refs[:count], refs[count:]
    if final:
        calls, extra, old = final
        mine, refs = refs[:extra], refs[extra:]
    if final:
        earlier, mine = mine[:old], mine[old:]
        block_ref, own_ref, rows_buf, own_buf, sem_own, blocks_buf, sem_out = refs
    else:
        blocks_buf, rows_buf = refs[:2]
    need = held.__getitem__
    need = held.__getitem__

    me, zi, xi, even = where_am_i()
    o_sib = jnp.where(even, 0, 2)
    roles = (1, o_sib, 2 - o_sib)
    base = len(used)
    near = [(i, at) for i in range(len(steps)) for at in range(n.inner)]
    order = [(role, i, at) for role, at in have for i in range(len(steps))]
    number = {key: g for g, key in enumerate(order)}
    cells = {
        (i, at): jnp.bitwise_xor(zi, steps[i]) * n.inner + jnp.bitwise_xor(xi, at) for i, at in near
    }
    u_at = {u: j for j, u in enumerate(used)}
    feat_of, tail_of = {}, {}
    for u in used:
        for i, b in enumerate(steps):
            tail_first = b > 1 and b % 2 == 1
            top, end = i * n.rows, (i + 1) * n.rows
            cut_at = top + (n.tail if tail_first else n.atoms)
            parts = need(u_at[u]).at[pl.ds(top, cut_at - top)], need(u_at[u]).at[pl.ds(cut_at, end - cut_at)]
            tail_of[u % 3, i, u // 3], feat_of[u % 3, i, u // 3] = parts if tail_first else parts[::-1]
    done = []

    def put(buf, at, order):
        for g, (role, b, beside) in enumerate(order):
            cell = jnp.bitwise_xor(zi, b) * n.inner + jnp.bitwise_xor(xi, beside)
            start = pl.multiple_of((roles[role] * n.cells + cell) * n.slot, n.slot)
            out = pltpu.make_async_copy(
                buf.at[:, pl.ds(g * n.slot, n.slot)],
                block_ref.at[:, pl.ds(start, n.slot)],
                sem_out.at[at + g],
            )
            out.start()
            done.append(out)

    if final and direct:
        sent = len(order)
        for buf, (planes, kinds) in zip(earlier, calls):
            spots = [(role, b, beside) for role, beside in kinds for b in planes]
            put(buf, sent, spots)
            sent += len(spots)
    if first:
        tails = [tail_of[role, 0, 0][...] for role in range(3)]
        table = refs[2]
        partner_table(n, even, feat_of[0, 0, 0][...], tails, need(base + 5)[...], table)
    else:
        table = need(base + 5)
    feats = jnp.concatenate([feat_of[key][...] for key in order], 0)
    left = dot(need(base)[...], feats, 1, 1).astype(BF16)

    slabs = []
    for role, i, at in order:
        top = (role * n.inner + at) * PLANES
        tail = tail_of[role, i, at][:, 0 : n.slot].astype(F32)
        slabs.append(tail[top : top + PLANES])
    meta = jnp.concatenate(slabs, 1)
    dists = meta[0:1] + meta[1:2] + meta[2:3]
    atoms = meta[3:4].astype(jnp.int32) - 1
    spots = meta[4:5].astype(jnp.int32)

    def cut(x, g):
        return x[:, g * n.slot : (g + 1) * n.slot]

    gate = gate_of(dists, need(base + 1)[...], need(base + 2)[...])
    rights = []
    for role in sorted({role for role, _ in have}):
        asking = [key for key in order if key[0] == role]
        place = [cut(spots, number[key]) + cells[key[1:]] * n.part for key in asking]
        rights.append(dot(table[role], onehot(jnp.concatenate(place, 1), n.cells * n.part)))
    lefts = [
        dot(left[:, g * n.atoms : (g + 1) * n.atoms], onehot(cut(atoms, g), n.atoms))
        for g in range(len(order))
    ]
    edge = jnp.concatenate(lefts, 1) * jnp.concatenate(rights, 1) * gate
    mixed = silu(dot(need(base + 3)[...], edge.astype(BF16))).astype(BF16)
    blocks_buf[...] = dot(need(base + 4)[...], mixed).astype(BF16)
    if final and direct:
        put(blocks_buf, 0, [(role, steps[i], at) for role, i, at in order])

    rows = len(order) * n.part
    my_list = lax.broadcasted_iota(jnp.int32, (n.cells, n.fetch), 0) == me
    index = []
    k = lax.broadcasted_iota(jnp.int32, (n.part, n.fetch), 1)
    m3 = 3 * lax.broadcasted_iota(jnp.int32, (n.part, n.fetch), 0)
    asked = {}
    for i, at in sorted({key[1:] for key in order}):
        lists = lists_of(n, tail_of[0, i, at][...])
        asked[i, at] = jnp.sum(jnp.where(my_list, lists, 0.0), 0, keepdims=True)
    for g, (role, i, at) in enumerate(order):
        o_own = 1 if role == 0 else 2 - roles[role]
        here = jnp.sum(jnp.where(k == m3 + o_own, asked[i, at], 0.0), 1, keepdims=True)
        index.append(here.astype(jnp.int32) + g * n.atoms)
    lane = lax.broadcasted_iota(jnp.int32, (rows, len(order) * n.atoms), 1)
    pick = (lane == jnp.concatenate(index, 0)).astype(BF16)
    rows_buf[...] = dot(pick, feats).astype(BF16)
    if final and not direct:
        out = pltpu.make_async_copy(blocks_buf, block_ref, sem_out.at[0])
        out.start()
        done.append(out)
    if final:
        w_mix = need(base + 3)
        done += own_part(n, calls, mine, w_mix, rows_buf, own_buf, own_ref, sem_own, even, zi, xi)
    for out in done:
        out.wait()


def received(n, steps, have, tiles, weights, table, w_right_t, own=None):
    first = table is None
    direct = n.slot % 128 == 0
    used = {u for role, at in have for u in (3 * at, 3 * at + role)}
    used = sorted(used | ({0, 1, 2} if first else set()))
    operands = [tiles[u] for u in used] + list(weights) + [w_right_t if first else table]
    count = len(operands)
    groups = len(have) * len(steps)
    blocks = (n.entries, groups * n.slot)
    rows = (groups * n.part, n.width)
    fast, slow = pl.BlockSpec(memory_space=pltpu.VMEM), pl.BlockSpec(memory_space=pl.ANY)
    final, scratch = None, []
    if own is None:
        out_shape = [jax.ShapeDtypeStruct(blocks, BF16), jax.ShapeDtypeStruct(rows, BF16)]
        out_specs = [fast, fast]
        if first:
            shape = (3, n.width, n.cells * n.part)
            out_shape.append(jax.ShapeDtypeStruct(shape, BF16))
            out_specs.append(fast)
    else:
        calls, earlier, extra = own
        total = 3 * n.cells
        operands += [*earlier, *extra]
        final = calls, len(operands) - count, len(earlier)
        shape = (n.entries, total * n.slot) if direct else blocks
        out_shape = [
            jax.ShapeDtypeStruct(shape, BF16),
            jax.ShapeDtypeStruct((n.entries, n.pairs), BF16),
        ]
        out_specs = [slow, slow]
        scratch = [
            pltpu.VMEM(rows, BF16),
            pltpu.VMEM((n.entries, n.pairs), BF16),
            pltpu.SemaphoreType.DMA((2,)),
            pltpu.VMEM(blocks, BF16),
            pltpu.SemaphoreType.DMA((total if direct else 1,)),
        ]
    return pl.pallas_call(
        functools.partial(received_kernel, n, steps, have, tuple(used), first, direct, count, final),
        in_specs=[fast] * len(operands),
        out_specs=out_specs,
        out_shape=out_shape,
        scratch_shapes=scratch,
        compiler_params=pltpu.CompilerParams(vmem_limit_bytes=LIMIT),
        cost_estimate=cost(500_000_000 * groups),
        name="received_blocks",
    )(*operands)


def own_part(n, calls, mine, w_mix, last, own_buf, own_ref, sem, even, zi, xi):
    place_ref, halves, w_right_ref, w_out_ref, tables = mine[0], mine[1:3], mine[3], mine[4], mine[5:]
    pieces = {}
    for (steps, have), found in zip(calls, (*tables, last)):
        keys = [(step, role, beside) for role, beside in have for step in steps]
        for g, key in enumerate(keys):
            pieces[key] = found[g * n.part : (g + 1) * n.part, :]
    rows = jnp.concatenate([pieces[key] for key in sorted(pieces)], 0)
    table = dot(w_right_ref[...], rows, 1, 1).astype(BF16)
    place = place_ref[...]
    done, at = [], 0
    for i, half in enumerate(halves):
        step = half.shape[1]
        right = dot(table, onehot(place[:, at : at + step], table.shape[1]))
        edge = (half[...] * right).astype(BF16)
        mixed = silu(dot(w_mix[...], edge)).astype(BF16)
        own_buf[:, at : at + step] = dot(w_out_ref[...], mixed).astype(BF16)
        part = pl.ds(at, step)
        out = pltpu.make_async_copy(own_buf.at[:, part], own_ref.at[:, part], sem.at[i])
        out.start()
        done.append(out)
        at += step
    return done


def body(
    features,
    pair_atom,
    partner_row,
    transpose_slot,
    distance,
    send_rows,
    w_left,
    w_right,
    w_radial_in,
    w_radial_out,
    w_mix,
    w_out,
):
    n = Sizes(features, pair_atom, send_rows, w_radial_in, w_out)
    lines = n.strips * n.cells

    def exchange(x, partner):
        pairs = []
        for i in range(lines):
            s, c = partner(i // n.cells, i % n.cells)
            pairs.append((i, s * n.cells + c))
        return lax.ppermute(x, AXES, pairs)

    def along(by):
        return lambda s, c: (s, c ^ (by * n.inner))

    def beside(s, c):
        return s, c ^ 1

    def sibling(s, c):
        return s ^ 1, c

    def other(s, c):
        return (s - 1 if s % 2 == 0 else s + 1) % n.strips, c

    row = lambda a: a.reshape(1, -1)
    pair_atom, partner_row = row(pair_atom), row(partner_row)
    transpose_slot, distance = row(transpose_slot), row(distance)
    tiles = make_tiles(
        n, pair_atom, partner_row, transpose_slot, distance, send_rows, features
    )
    lines_in = {0: tiles[0]}
    for b, tile in zip(sent_steps(n), tiles):
        if b:
            lines_in[b] = exchange(tile, along(b))
    for b in range(3, n.outer, 2):
        lines_in[b] = exchange(lines_in[b - 1], along(1))
    step = n.pairs // 2
    held, turned, left, w_out_t = first_gate(
        n,
        step,
        distance,
        pair_atom,
        features,
        (w_left, w_right, w_radial_in, w_radial_out, w_mix, w_out.T),
    )
    second, place = second_gate(
        n, step, distance, pair_atom, partner_row, left, turned[2], turned[3]
    )
    lines_in[1], lines_in[2], second = lax.optimization_barrier((lines_in[1], lines_in[2], second))
    w_left_t, w_right_t, w_in_t, w_ro_t, w_mix_t, w_flip_t = turned
    weights = (w_left_t, w_in_t, w_ro_t, w_mix_t, w_flip_t)
    tables, parts, calls = [], [], []

    def take(at, have, table):
        steps, group = sets[at]
        blocks, rows, *new = received(n, steps, have, group, weights, table, w_right_t)
        tables.append(rows)
        parts.append(blocks)
        calls.append((steps, have))
        return new[0] if new else table

    sets, chain = [], []
    for b in range(0, n.outer, 2):
        tile = jnp.concatenate([lines_in[b][-n.rows :], lines_in[b + 1][: n.rows]], 0)
        chain.append([tile, exchange(tile, sibling), exchange(tile, other), exchange(tile, beside)])
    for i, (tile, close, away, across) in enumerate(chain):
        corner_tile = exchange(across, other) if i % 2 else exchange(away, beside)
        group = [tile, close, away, across, exchange(across, sibling), corner_tile]
        sets.append(((2 * i, 2 * i + 1), group))
    last, table = len(sets) - 1, None
    same_strips, away_near, away_far = ((0, 0), (0, 1), (1, 0), (1, 1)), ((2, 0),), ((2, 1),)
    for i in range(last + 1):
        table = take(i, same_strips, table)
    for i in range(last):
        table = take(i, away_near + away_far, table)
    table = take(last, away_near, table)
    every = (*calls, (sets[last][0], away_far))
    earlier = parts if n.slot % 128 == 0 else []
    own = (every, earlier, [place, held, second, w_right_t, w_out_t, *tables])
    into, own = received(n, sets[last][0], away_far, sets[last][1], weights, table, w_right_t, own)
    if n.slot % 128:
        cell, strip = lax.axis_index("cell"), lax.axis_index("strip")
        o_sib = jnp.where(strip % 2 == 0, 0, 2)
        parts.append(into)
        into = jnp.zeros((n.entries, 3 * n.cells * n.slot), BF16)
        for (steps, have), blocks in zip(every, parts):
            order = [(role, b, at) for role, at in have for b in steps]
            for g, (role, b, at) in enumerate(order):
                piece = blocks[:, g * n.slot : (g + 1) * n.slot]
                spot = (1, o_sib, 2 - o_sib)[role] * n.cells + (cell ^ (b * n.inner + at))
                into = lax.dynamic_update_slice(into, piece, (0, spot * n.slot))
    return own, into


def solution(mesh):
    split = P(("strip", "cell"))
    wide = P(("strip", "cell"), None)
    in_specs = (wide, split, split, split, split, wide) + (P(),) * 6
    out_specs = (P(None, ("strip", "cell")), P(None, ("strip", "cell")))
    return jax.shard_map(body, mesh=mesh, in_specs=in_specs, out_specs=out_specs, check_vma=False)
```
